32 devices in a mesh: dp: 8 (over y, x, core), ctx: 4 (over z).
Axes of the slice: x: 2, y: 2, z: 4, core: 2. Of those that a mesh axis runs over, the one named last changes fastest.
Arguments:
- q_src: bfloat16 [4096, 4096], P(('dp', 'ctx')), may hold values from -40 to 40
- kv_src: bfloat16 [4096, 1024], P(('dp', 'ctx')), may hold values from -40 to 40
- route: int32 [4096, 1], replicated, may hold values from 0 to 7; in each aligned block of 512 rows (0 to 511, 512 to 1023, ...) at most 96 rows name the same one
- doc_ids: int32 [8, 768], P('dp'), may hold values from 0 to 5, never falling along the last dimension, each value on 1 to 256 neighbouring positions
Outputs:
- attended: bfloat16 [6144, 4096], P(('dp', 'ctx'))
The draws below stay inside these ranges and needn't reach their ends.
Inputs may be any that keep to these rules, and one draw needn't show every extreme that they name: `route`: within each source group's 512 rows (aligned blocks of 512 rows), no sequence is named by more than 96 rows, a bound that some block reaches. `doc_ids`: never falling along a sequence; every document has 1 to 256 slots and one has exactly 256.
All inputs are finite; a program needn't handle non-finite values.
Results may differ from the reference program's by a relative error of at most 0.011.
Values may be sent and summed in bfloat16 or wider, within the bound.
No kernel may reach another device: no remote copies, remote signals or barrier semaphores. Data moves between devices by JAX's collectives and lax.ppermute only.
A program may use at most 64 MiB of HBM per device.

```python
import math
import jax
import jax.numpy as jnp
import numpy as np
from jax import lax

Q_HEADS = 32
KV_HEADS = 4
HEAD_DIM = 128
SEQS = 8
L = 512
CAP = 96
PACK = 768
DOC_MOST = 256
DOCS = 6


def draw_q_src(key, part):
    row_count = SEQS * L
    group_size = Q_HEADS // KV_HEADS
    base_draw = jax.random.normal(jax.random.fold_in(key, 1), (row_count, KV_HEADS, group_size, HEAD_DIM), jnp.float32)
    base_draw = jnp.clip(base_draw, -5.0, 5.0)
    return jnp.clip(base_draw, -40.0, 40.0).reshape(row_count, Q_HEADS * HEAD_DIM).astype(jnp.bfloat16)


def draw_kv_src(key, part):
    row_count = SEQS * L
    base_draw = jax.random.normal(jax.random.fold_in(key, 5), (row_count, 2, KV_HEADS, HEAD_DIM), jnp.float32)
    base_draw = jnp.clip(base_draw, -5.0, 5.0)
    return jnp.clip(base_draw, -40.0, 40.0).reshape(row_count, 2 * KV_HEADS * HEAD_DIM).astype(jnp.bfloat16)


def profile(number_of, total, bound, slope):
    weights = [(1 << 20) // math.isqrt(grade ** slope) + 1 for grade in range(2, number_of + 1)]
    surplus, counts = total - bound - (number_of - 1), [1] * (number_of - 1)
    while surplus > 0:
        free = [i for i in range(number_of - 1) if counts[i] < bound]
        pool, remaining = sum([weights[i] for i in free]), surplus
        for i in free:
            extra = min(bound - counts[i], max(1, remaining * weights[i] // pool), surplus)
            counts[i] = counts[i] + extra
            surplus = surplus - extra
    return np.array([bound] + counts)


def ragged(own_key, number_of, total, most, slope):
    if number_of == 2:
        one = jax.random.randint(own_key, (), max(1, total - most), min(most, total - 1) + 1)
        return jnp.stack([one, total - one])
    sizes = jnp.asarray(profile(number_of, total, most, slope), jnp.int32)
    pairs = (number_of - 1) // 2
    source_of, sink = sizes[1:1 + 2 * pairs:2], sizes[2:2 + 2 * pairs:2]
    slack = jnp.minimum(source_of - 1, most - sink)
    moved = jax.random.randint(jax.random.fold_in(own_key, 1), (pairs,), 0, 1 << 20) % (slack + 1)
    sizes = sizes.at[1:1 + 2 * pairs:2].set(source_of - moved).at[2:2 + 2 * pairs:2].set(sink + moved)
    return sizes[jax.random.permutation(jax.random.fold_in(own_key, 2), number_of)]


def routed_block(rng, own, number, rows, amount, top, bound, skew):
    sequence = jax.random.permutation(rng, amount)
    crowded, usual = shares(amount, rows * top, bound, skew, True), shares(amount, rows * top, bound, skew, False)
    places = jnp.arange(amount)

    def named(tallies, rotation):
        used = int((tallies > 0).sum())
        fixed = max(1, used // 4)
        shifted = fixed + (places - fixed + rotation * (used - fixed)) % max(1, amount - fixed)
        return jnp.zeros((amount,), jnp.int32).at[sequence[jnp.where(places < fixed, places, shifted)]].set(jnp.asarray(tallies, jnp.int32))

    tallies = jnp.where(number % 4 == 0, named(crowded, number // 4), named(usual, number - number // 4 - 1))
    mixed = jax.random.permutation(jax.random.fold_in(own, 3), amount)
    giver, sink = mixed[0:amount // 2 * 2:2], mixed[1:amount // 2 * 2:2]
    room = jnp.minimum(tallies[giver] - 1, bound - tallies[sink]) // 2
    room = jnp.where((giver == sequence[0]) | (sink == sequence[0]) | (tallies[sink] == 0), 0, jnp.maximum(room, 0))
    shifted = jax.random.randint(jax.random.fold_in(own, 4), (amount // 2,), 0, 1 << 20) % (room + 1)
    tallies = tallies.at[giver].add(-shifted).at[sink].add(shifted)
    labels = jnp.searchsorted(jnp.cumsum(tallies), jnp.arange(rows * top), side="right").astype(jnp.int32)
    grid = labels.reshape(top, rows).T
    grid = grid[jax.random.permutation(jax.random.fold_in(own, 1), rows)]
    rotation = jax.random.randint(jax.random.fold_in(own, 2), (rows, 1), 0, top)
    return jnp.take_along_axis(grid, (jnp.arange(top)[None, :] + rotation) % top, axis=1)


def shares(count, total, most, skew, full):
    loads = [(1 << 20) // math.isqrt(rank ** skew) + 1 for rank in range(1, count + 1)]
    largest = most if full else min(most, max(-(-total // count), total * loads[0] // sum(loads)))
    least = 1 if total - largest >= count - 1 else 0
    holding, spare = [largest] + [least] * (count - 1), total - largest - least * (count - 1)
    while spare > 0:
        free = [i for i in range(1, count) if holding[i] < largest] or [i for i in range(1, count) if holding[i] < most]
        whole, left = sum([loads[i] for i in free]), spare
        for i in free:
            extra = min(most - holding[i], max(1, left * loads[i] // whole), spare)
            holding[i] = holding[i] + extra
            spare = spare - extra
    return np.array(holding)


def setup_inputs(seed: int = 0) -> dict:
    splits = jax.random.split(jax.random.key(seed), 5)
    q_src = draw_q_src(jax.random.fold_in(splits[4], 71), 0)
    kv_src = draw_kv_src(jax.random.fold_in(splits[4], 71), 0)
    route_keys = jax.random.split(jax.random.fold_in(splits[2], 1), (SEQS * L) // L)
    route_turns = jax.random.permutation(jax.random.fold_in(splits[2], 3), (SEQS * L) // L)
    route = jax.vmap(lambda own, number: routed_block(jax.random.fold_in(splits[2], 2), own, number, L, SEQS, 1, CAP, 1))(route_keys, route_turns).reshape((SEQS * L, 1))
    doc_ids = jax.vmap(lambda own: jnp.searchsorted(jnp.cumsum(ragged(own, DOCS, PACK, DOC_MOST, 2)), jnp.arange(PACK), side="right"))(jax.random.split(splits[3], SEQS)).reshape((SEQS, PACK)).astype(jnp.int32)
    return {"q_src": q_src, "kv_src": kv_src, "route": route, "doc_ids": doc_ids}


def attend(queries, kv_pairs, doc_rows, live_rows, kv_local):
    pack_len = queries.shape[0]
    head_count = queries.shape[1] // HEAD_DIM
    group_size = head_count // kv_local
    block_len = math.gcd(pack_len, 512)
    window = min(pack_len, DOC_MOST + block_len)
    score_scale = HEAD_DIM ** -0.5
    grouped = queries.reshape(pack_len, kv_local, group_size, HEAD_DIM)
    split_pairs = kv_pairs.reshape(pack_len, 2, kv_local, HEAD_DIM)

    def one_block(block_index):
        row_start = block_index * block_len
        key_start = jnp.maximum(row_start + block_len - window, 0)
        query_block = lax.dynamic_slice_in_dim(grouped, row_start, block_len, 0).astype(jnp.float32)
        key_block = lax.dynamic_slice_in_dim(split_pairs, key_start, window, 0).astype(jnp.float32)
        query_docs = lax.dynamic_slice_in_dim(doc_rows, row_start, block_len, 0)
        key_docs = lax.dynamic_slice_in_dim(doc_rows, key_start, window, 0)
        query_pos = row_start + jnp.arange(block_len, dtype=jnp.int32)
        key_pos = key_start + jnp.arange(window, dtype=jnp.int32)
        allowed = (query_docs[:, None] == key_docs[None, :]) & (key_pos[None, :] <= query_pos[:, None])
        scores = jnp.einsum("qkgd,skd->kgqs", query_block, key_block[:, 0]) * score_scale
        masked = jnp.where(allowed, scores, -1e30)
        row_max = jnp.max(masked, axis=-1, keepdims=True)
        exponent = jnp.where(allowed, jnp.exp(masked - row_max), 0.0)
        probs = exponent / jnp.sum(exponent, axis=-1, keepdims=True)
        weights = probs.astype(jnp.bfloat16)
        mixed = jnp.einsum("kgqs,skd->qkgd", weights.astype(jnp.float32), key_block[:, 1])
        mixed = jnp.where((query_pos < live_rows)[:, None, None, None], mixed, 0.0)
        return mixed.astype(jnp.bfloat16).reshape(block_len, head_count * HEAD_DIM)

    blocks = lax.map(one_block, jnp.arange(pack_len // block_len, dtype=jnp.int32))
    return blocks.reshape(pack_len, head_count * HEAD_DIM)


def reference(q_src, kv_src, route, doc_ids):
    plan_rows = route.reshape(-1).astype(jnp.int32)
    seq_ids = jnp.arange(SEQS, dtype=jnp.int32)
    onehot = (plan_rows[:, None] == seq_ids[None, :]).astype(jnp.int32)
    before = (jnp.cumsum(onehot, axis=0) - onehot).astype(jnp.int32)
    position = jnp.sum(before * onehot, axis=1).astype(jnp.int32)
    totals = jnp.sum(onehot, axis=0).astype(jnp.int32)
    flat_slot = (plan_rows * PACK + position).astype(jnp.int32)
    packed_q = jnp.zeros((SEQS * PACK, q_src.shape[1]), jnp.bfloat16).at[flat_slot].set(q_src)
    packed_kv = jnp.zeros((SEQS * PACK, kv_src.shape[1]), jnp.bfloat16).at[flat_slot].set(kv_src)

    def per_sequence(items):
        seq_q, seq_kv, seq_docs, live_rows = items
        return attend(seq_q, seq_kv, seq_docs, live_rows, KV_HEADS)

    result = lax.map(per_sequence, (packed_q.reshape(SEQS, PACK, -1), packed_kv.reshape(SEQS, PACK, -1), doc_ids, totals))
    return result.reshape(SEQS * PACK, Q_HEADS * HEAD_DIM)
```

```python
import functools
import math

import jax
import jax.numpy as jnp
from jax import lax
from jax.experimental import pallas as pl
from jax.experimental.pallas import tpu as pltpu
from jax.sharding import PartitionSpec as P

Q_HEADS = 32
KV_HEADS = 4
HEAD_DIM = 128
BLOCK = 128
VMEM_LIMIT = 40 * 1024 * 1024
ANY = pl.BlockSpec(memory_space=pl.ANY)


def params():
    return pltpu.CompilerParams(vmem_limit_bytes=VMEM_LIMIT)


def cost(flops, moved, exps=0):
    return pl.CostEstimate(flops=int(flops), bytes_accessed=int(moved), transcendentals=int(exps))


def head_chunks(heads_dev):
    first = max(1, heads_dev // 4)
    second = (heads_dev - first + 1) // 2
    sizes = [first, second, heads_dev - first - second]
    chunks, start = [], 0
    for size in sizes:
        if size:
            chunks.append((start, size))
            start += size
    return chunks


def cut_kernel(chunks, ctx_size, with_kv, q_ref, kv_ref, *refs):
    outs, sem = refs[:-1], refs[-1]
    me = lax.axis_index("ctx")
    heads_dev = Q_HEADS // ctx_size
    group = Q_HEADS // KV_HEADS
    copies = []
    for at, (offset, heads) in enumerate(chunks):
        wide = heads * HEAD_DIM
        for step in list(range(1, ctx_size)) + [0]:
            owner = me ^ step
            out = outs[at * ctx_size + step]
            column = pl.multiple_of((owner * heads_dev + offset) * HEAD_DIM, HEAD_DIM)
            copies.append((q_ref.at[:, pl.ds(column, wide)], out.at[:, pl.ds(0, wide)]))
            if with_kv and at == 0:
                head = (owner * heads_dev) // group
                for half in range(2):
                    column = pl.multiple_of((half * KV_HEADS + head) * HEAD_DIM, HEAD_DIM)
                    copies.append(
                        (
                            kv_ref.at[:, pl.ds(column, HEAD_DIM)],
                            out.at[:, pl.ds(wide + half * HEAD_DIM, HEAD_DIM)],
                        )
                    )
    started = [pltpu.make_async_copy(a, b, sem.at[i]) for i, (a, b) in enumerate(copies)]
    for copy in started:
        copy.start()
    for copy in started:
        copy.wait()


def cut(q_src, kv_src, chunks, ctx_size, with_kv):
    rows = q_src.shape[0]
    shapes, number = [], 0
    for at, (_, heads) in enumerate(chunks):
        extra = 2 * HEAD_DIM if with_kv and at == 0 else 0
        number += ctx_size * (3 if extra else 1)
        shapes += [jax.ShapeDtypeStruct((rows, heads * HEAD_DIM + extra), jnp.bfloat16)] * ctx_size
    moved = 4 * sum([math.prod(s.shape) for s in shapes])
    outs = pl.pallas_call(
        functools.partial(cut_kernel, chunks, ctx_size, with_kv),
        out_shape=shapes,
        in_specs=[ANY, ANY],
        out_specs=[ANY] * len(shapes),
        scratch_shapes=[pltpu.SemaphoreType.DMA((number,))],
        compiler_params=params(),
        cost_estimate=cost(0, moved),
    )(q_src, kv_src)
    return [outs[i : i + ctx_size] for i in range(0, len(shapes), ctx_size)]


def swap(blocks, axis, size):
    return [blocks[0]] + [
        lax.ppermute(blocks[step], axis, [(j, j ^ step) for j in range(size)])
        for step in range(1, size)
    ]


def plan_kernel(capacity, ctx_size, route_ref, target_ref, slot_ref, live_ref, tmp):
    dp_size, length = route_ref.shape
    rows = length // ctx_size
    pack_len = dp_size * capacity
    own, me = lax.axis_index("dp"), lax.axis_index("ctx")
    mine = route_ref[pl.ds(own, 1), :]
    seq = lax.broadcasted_iota(jnp.int32, (dp_size, length), 0)
    onehot = jnp.where(mine == seq, 1.0, 0.0)
    earlier = lax.broadcasted_iota(jnp.int32, (length, length), 0)
    later = lax.broadcasted_iota(jnp.int32, (length, length), 1)
    strict = jnp.where(earlier < later, 1.0, 0.0).astype(jnp.bfloat16)
    before = jnp.dot(onehot.astype(jnp.bfloat16), strict, preferred_element_type=jnp.float32)
    rank = jnp.sum(before * onehot, axis=0, keepdims=True).astype(jnp.int32)
    tmp[...] = mine * capacity + rank
    for step in range(ctx_size):
        source = me ^ step
        target_ref[:, pl.ds(step * rows, rows)] = tmp[
            :, pl.ds(pl.multiple_of(source * rows, rows), rows)
        ]
    incoming = jnp.sum(
        jnp.where(route_ref[...] == own, 1.0, 0.0), axis=1, keepdims=True
    )
    group = lax.broadcasted_iota(jnp.int32, (dp_size, pack_len), 0)
    lane = lax.broadcasted_iota(jnp.int32, (dp_size, pack_len), 1)
    first = group * capacity
    inside = (lane >= first) & (lane < first + capacity)
    start = jnp.sum(jnp.where(lane >= first + capacity, incoming, 0.0), axis=0, keepdims=True)
    amount = jnp.sum(jnp.where(inside, incoming, 0.0), axis=0, keepdims=True).astype(jnp.int32)
    offset = jnp.sum(jnp.where(inside, lane - first, 0), axis=0, keepdims=True)
    slot_ref[...] = jnp.where(offset < amount, start.astype(jnp.int32) + offset, -1)
    live = jnp.sum(incoming, axis=0, keepdims=True).astype(jnp.int32)
    live_ref[...] = jnp.broadcast_to(live, live_ref.shape)


def plan(route, dp_size, ctx_size, capacity):
    length = route.shape[0] // dp_size
    return pl.pallas_call(
        functools.partial(plan_kernel, capacity, ctx_size),
        out_shape=[
            jax.ShapeDtypeStruct((1, length), jnp.int32),
            jax.ShapeDtypeStruct((1, dp_size * capacity), jnp.int32),
            jax.ShapeDtypeStruct((1, HEAD_DIM), jnp.int32),
        ],
        scratch_shapes=[pltpu.VMEM((1, length), jnp.int32)],
        compiler_params=params(),
        cost_estimate=cost(2 * dp_size * length * length, 8 * length * dp_size),
    )(route.reshape(dp_size, length))


def pack_kernel(capacity, target_ref, *refs):
    blocks, out_ref = refs[:-1], refs[-1]
    dp_size = out_ref.shape[0]
    length = target_ref.shape[1]
    together = math.gcd(dp_size, 8)
    data = jnp.concatenate([b[...] for b in blocks], axis=0)
    target = target_ref[...]
    high = together * capacity
    row = lax.broadcasted_iota(jnp.int32, (high, length), 0)
    for part in range(dp_size // together):
        place = jnp.where(target == row + part * high, 1.0, 0.0).astype(jnp.bfloat16)
        packed = jnp.dot(place, data, preferred_element_type=jnp.float32).astype(jnp.bfloat16)
        out_ref[part * together : (part + 1) * together] = packed.reshape(
            together, capacity, data.shape[1]
        )


def pack(target, blocks, dp_size, capacity):
    wide = blocks[0].shape[1]
    length = target.shape[1]
    size = dp_size * capacity * wide
    return pl.pallas_call(
        functools.partial(pack_kernel, capacity),
        out_shape=jax.ShapeDtypeStruct((dp_size, capacity, wide), jnp.bfloat16),
        compiler_params=params(),
        cost_estimate=cost(2 * size * length, 2 * size + 2 * length * wide),
    )(target, *blocks)


def attend_kernel(heads, doc_most, ctx_size, with_kv, recv_ref, slot_ref, live_ref, doc_ref, col_ref, *refs):
    if with_kv:
        outs, (kv_ref, acc) = refs[:ctx_size], refs[ctx_size:]
    else:
        kv_ref, outs, acc = refs[0], refs[1 : 1 + ctx_size], refs[1 + ctx_size]
    me = lax.axis_index("ctx")
    pack_len = acc.shape[0]
    wide = heads * HEAD_DIM
    scale = HEAD_DIM ** (-0.5) * math.log2(math.e)
    window = min(pack_len, doc_most + BLOCK)
    row = lax.broadcasted_iota(jnp.int32, (BLOCK, pack_len), 0)
    slot = slot_ref[...]
    live = live_ref[...]
    ones = jnp.ones((window, HEAD_DIM), jnp.bfloat16)
    received = recv_ref[...]
    for block in range(pack_len // BLOCK):
        begin = block * BLOCK
        rows = pl.ds(begin, BLOCK)
        place = jnp.where(slot == row + begin, 1.0, 0.0).astype(jnp.bfloat16)
        packed = jnp.dot(place, received, preferred_element_type=jnp.float32).astype(jnp.bfloat16)
        if with_kv:
            kv_ref[rows, :] = packed[:, wide:]
        key_start = max(0, begin + BLOCK - window)
        span = begin + BLOCK - key_start
        keys = kv_ref[pl.ds(key_start, span), :HEAD_DIM]
        values = jnp.concatenate([kv_ref[pl.ds(key_start, span), HEAD_DIM:], ones[:span]], axis=1)
        query_pos = begin + lax.broadcasted_iota(jnp.int32, (BLOCK, span), 0)
        key_pos = key_start + lax.broadcasted_iota(jnp.int32, (BLOCK, span), 1)
        docs = jnp.concatenate([col_ref[rows, :]] * (span // HEAD_DIM), axis=1)
        allowed = (docs == doc_ref[:, pl.ds(key_start, span)]) & (key_pos <= query_pos)
        alive = begin + lax.broadcasted_iota(jnp.int32, (BLOCK, HEAD_DIM), 0) < live
        for head in range(heads):
            query = packed[:, head * HEAD_DIM : (head + 1) * HEAD_DIM]
            scores = lax.dot_general(
                query, keys, (((1,), (1,)), ((), ())), preferred_element_type=jnp.float32
            )
            masked = jnp.where(allowed, scores, -1e30)
            top = jnp.max(masked, axis=1, keepdims=True)
            weights = jnp.exp2((masked - top) * scale).astype(jnp.bfloat16)
            mixed = jnp.dot(weights, values, preferred_element_type=jnp.float32)
            result = mixed[:, :HEAD_DIM] / mixed[:, HEAD_DIM:]
            acc[rows, head * HEAD_DIM : (head + 1) * HEAD_DIM] = jnp.where(
                alive, result, 0.0
            ).astype(jnp.bfloat16)
    part = pack_len // ctx_size
    for step in range(ctx_size):
        first = pl.multiple_of((me ^ step) * part, part)
        outs[step][...] = acc[pl.ds(first, part), :]


def attend(recv, slot, live, doc_row, doc_col, kv, heads, ctx_size):
    pack_len = recv.shape[0]
    doc_most = pack_len // 3
    wide = heads * HEAD_DIM
    with_kv = kv is None
    shapes = [jax.ShapeDtypeStruct((pack_len // ctx_size, wide), jnp.bfloat16)] * ctx_size
    if with_kv:
        shapes = shapes + [jax.ShapeDtypeStruct((pack_len, 2 * HEAD_DIM), jnp.bfloat16)]
    work = pack_len * (doc_most + BLOCK) * heads
    outs = pl.pallas_call(
        functools.partial(attend_kernel, heads, doc_most, ctx_size, with_kv),
        out_shape=shapes,
        scratch_shapes=[pltpu.VMEM((pack_len, wide), jnp.bfloat16)],
        compiler_params=params(),
        cost_estimate=cost(
            2 * pack_len * pack_len * recv.shape[1] + 6 * work * HEAD_DIM, 8 * pack_len * wide, work
        ),
    )(recv, slot, live, doc_row, doc_col, *([] if with_kv else [kv]))
    return list(outs[:ctx_size]), (outs[ctx_size] if with_kv else kv)


def join_kernel(chunk, ctx_size, first, *refs):
    offset, heads = chunk
    heads_dev = Q_HEADS // ctx_size
    blocks = refs[:ctx_size]
    out, sem = refs[-2:]
    me = lax.axis_index("ctx")
    copies = []
    for step in range(ctx_size):
        column = pl.multiple_of(((me ^ step) * heads_dev + offset) * HEAD_DIM, HEAD_DIM)
        copies.append(
            pltpu.make_async_copy(
                blocks[step], out.at[:, pl.ds(column, heads * HEAD_DIM)], sem.at[step]
            )
        )
    for copy in copies:
        copy.start()
    for copy in copies:
        copy.wait()


def join(blocks, chunk, out, ctx_size):
    rows = blocks[0].shape[0]
    given = [] if out is None else [out]
    return pl.pallas_call(
        functools.partial(join_kernel, chunk, ctx_size, out is None),
        out_shape=jax.ShapeDtypeStruct((rows, Q_HEADS * HEAD_DIM), jnp.bfloat16),
        in_specs=[ANY] * (ctx_size + len(given)),
        out_specs=ANY,
        scratch_shapes=[pltpu.SemaphoreType.DMA((ctx_size,))],
        input_output_aliases={ctx_size: 0} if given else {},
        compiler_params=params(),
        cost_estimate=cost(0, 4 * rows * chunk[1] * HEAD_DIM * ctx_size),
    )(*blocks, *given)


def on_device(q_src, kv_src, route, doc_ids):
    ctx_size = lax.axis_size("ctx")
    dp_size = lax.axis_size("dp")
    length = q_src.shape[0] * ctx_size
    capacity = 3 * length // (2 * dp_size)
    pack_len = dp_size * capacity
    chunks = head_chunks(Q_HEADS // ctx_size)

    cuts = cut(q_src, kv_src, chunks[:1], ctx_size, True)
    if chunks[1:]:
        cuts = cuts + cut(q_src, kv_src, chunks[1:], ctx_size, False)
    gathered = [swap(blocks, "ctx", ctx_size) for blocks in cuts]
    target, slot, live = plan(route, dp_size, ctx_size, capacity)
    doc_col = jnp.broadcast_to(doc_ids.reshape(pack_len, 1), (pack_len, HEAD_DIM))

    received = []
    for blocks in gathered:
        sent = pack(target, blocks, dp_size, capacity)
        got = lax.all_to_all(sent, "dp", split_axis=0, concat_axis=0, tiled=True)
        received.append(got.reshape(pack_len, -1))

    kv, out = None, None
    for chunk, recv in zip(chunks, received):
        blocks, kv = attend(recv, slot, live, doc_ids, doc_col, kv, chunk[1], ctx_size)
        out = join(swap(blocks, "ctx", ctx_size), chunk, out, ctx_size)
    return out


def solution(mesh):
    in_specs = (P(("dp", "ctx"), None), P(("dp", "ctx"), None), P(), P("dp", None))
    out_specs = P(("dp", "ctx"), None)
    return jax.shard_map(
        on_device, mesh=mesh, in_specs=in_specs, out_specs=out_specs, check_vma=False
    )
```

```python
import functools
import math

import jax
import jax.numpy as jnp
from jax import lax
from jax.experimental import pallas as pl
from jax.experimental.pallas import tpu as pltpu
from jax.sharding import PartitionSpec as P

Q_HEADS = 32
KV_HEADS = 4
HEAD_DIM = 128
BLOCK = 128
VMEM_LIMIT = 40 * 1024 * 1024
SHARES = [[4], [4]]
SWAPS = 2
D1 = False
PIN_OTHER = True
PIN_PACK = ()
D3 = (1,)
PIN_SENT = ()
PIN_OLD = ()
STACK_IN = ()
STACK_OUT = (0,)
CUT_LIMIT = 66 * 1024 * 1000
ANY = pl.BlockSpec(memory_space=pl.ANY)
HBM = pl.BlockSpec(memory_space=pltpu.HBM)
VMEM = pl.BlockSpec(memory_space=pltpu.VMEM)


def params(limit=VMEM_LIMIT):
    return pltpu.CompilerParams(vmem_limit_bytes=limit)


def cost(flops, moved, exps=0):
    return pl.CostEstimate(flops=int(flops), bytes_accessed=int(moved), transcendentals=int(exps))


def head_chunks(heads_dev):
    pieces, start = [], 0
    for piece in SHARES:
        chunks = []
        for share in piece:
            size = min(max(1, share * heads_dev // 8), heads_dev - start)
            if size:
                chunks.append((start, size))
                start += size
        if chunks:
            pieces.append(chunks)
    return pieces


def cut_kernel(piece, ctx_size, with_kv, stacked, waits, q_ref, kv_ref, *refs):
    outs, sem = refs[waits:-1], refs[-1]
    me = lax.axis_index("ctx")
    heads_dev = Q_HEADS // ctx_size
    group = Q_HEADS // KV_HEADS
    copies = []
    for step in list(range(1, ctx_size)) + [0]:
        owner = step if stacked else me ^ step
        out = outs[0].at[step] if stacked else outs[step]
        parts = [(q_ref, owner * heads_dev + piece[0][0], sum([chunk[1] for chunk in piece]))]
        if with_kv:
            head = (owner * heads_dev) // group
            first = piece[0][1]
            parts = [
                (q_ref, owner * heads_dev + piece[0][0], first),
                (kv_ref, head, 1),
                (kv_ref, KV_HEADS + head, 1),
                (q_ref, owner * heads_dev + piece[0][0] + first, parts[0][2] - first),
            ]
        place = 0
        for source, block, number in parts:
            if number:
                wide = number * HEAD_DIM
                column = pl.multiple_of(block * HEAD_DIM, HEAD_DIM)
                copies.append(
                    (source.at[:, pl.ds(column, wide)], out.at[:, pl.ds(place, wide)])
                )
                place += wide
    started = [pltpu.make_async_copy(a, b, sem.at[i]) for i, (a, b) in enumerate(copies)]
    for copy in started:
        copy.start()
    for copy in started:
        copy.wait()


def cut(q_src, kv_src, piece, ctx_size, with_kv, stacked, after, limit):
    rows = q_src.shape[0]
    wide = (sum([chunk[1] for chunk in piece]) + (2 if with_kv else 0)) * HEAD_DIM
    if stacked:
        shapes = [jax.ShapeDtypeStruct((ctx_size, rows, wide), jnp.bfloat16)]
    else:
        shapes = [jax.ShapeDtypeStruct((rows, wide), jnp.bfloat16)] * ctx_size
    number = ctx_size * ((4 if len(piece) > 1 else 3) if with_kv else 1)
    outs = pl.pallas_call(
        functools.partial(cut_kernel, piece, ctx_size, with_kv, stacked, len(after)),
        out_shape=shapes,
        in_specs=[ANY] * (2 + len(after)),
        out_specs=[VMEM] * len(shapes),
        scratch_shapes=[pltpu.SemaphoreType.DMA((number,))],
        compiler_params=params(limit),
        cost_estimate=cost(0, 4 * ctx_size * rows * wide),
    )(q_src, kv_src, *after)
    return list(outs)


def swap(blocks, axis, size, unit=1):
    return [blocks[0]] + [
        lax.ppermute(blocks[step], axis, [(j, j ^ (step * unit)) for j in range(size)])
        for step in range(1, len(blocks))
    ]


def exchange(blocks, ctx_size):
    if len(blocks) == 1:
        return [lax.all_to_all(blocks[0], "ctx", split_axis=0, concat_axis=0, tiled=True)]
    return swap(blocks, "ctx", ctx_size)


def plan_kernel(capacity, ctx_size, route_ref, target_ref, swapped_ref, slot_ref, live_ref):
    dp_size, length = route_ref.shape
    rows = length // ctx_size
    pack_len = dp_size * capacity
    own, me = lax.axis_index("dp"), lax.axis_index("ctx")
    mine = route_ref[pl.ds(own, 1), :]
    seq = lax.broadcasted_iota(jnp.int32, (dp_size, length), 0)
    onehot = jnp.where(mine == seq, 1.0, 0.0)
    earlier = lax.broadcasted_iota(jnp.int32, (length, length), 0)
    later = lax.broadcasted_iota(jnp.int32, (length, length), 1)
    strict = jnp.where(earlier < later, 1.0, 0.0).astype(jnp.bfloat16)
    before = jnp.dot(onehot.astype(jnp.bfloat16), strict, preferred_element_type=jnp.float32)
    rank = jnp.sum(before * onehot, axis=0, keepdims=True).astype(jnp.int32)
    other = mine ^ own
    place = (other & 1) * (dp_size // 2) + (other >> 1)
    target_ref[...] = place * capacity + rank
    for step in range(ctx_size):
        source = me ^ step
        swapped_ref[:, pl.ds(step * rows, rows)] = target_ref[
            :, pl.ds(pl.multiple_of(source * rows, rows), rows)
        ]
    incoming = jnp.sum(
        jnp.where(route_ref[...] == own, 1.0, 0.0), axis=1, keepdims=True
    )
    group = lax.broadcasted_iota(jnp.int32, (dp_size, pack_len), 0)
    lane = lax.broadcasted_iota(jnp.int32, (dp_size, pack_len), 1)
    block = lax.div(lane, capacity)
    source = block ^ own
    start = jnp.sum(jnp.where(group < source, incoming, 0.0), axis=0, keepdims=True)
    amount = jnp.sum(jnp.where(group == source, incoming, 0.0), axis=0, keepdims=True)
    offset = (lane - block * capacity)[:1]
    slot_ref[...] = jnp.where(
        offset < amount.astype(jnp.int32), start.astype(jnp.int32) + offset, -1
    )
    live = jnp.sum(incoming, axis=0, keepdims=True).astype(jnp.int32)
    live_ref[...] = jnp.broadcast_to(live, live_ref.shape)


def plan(route, dp_size, ctx_size, capacity):
    length = route.shape[0] // dp_size
    return pl.pallas_call(
        functools.partial(plan_kernel, capacity, ctx_size),
        out_shape=[
            jax.ShapeDtypeStruct((1, length), jnp.int32),
            jax.ShapeDtypeStruct((1, length), jnp.int32),
            jax.ShapeDtypeStruct((1, dp_size * capacity), jnp.int32),
            jax.ShapeDtypeStruct((1, HEAD_DIM), jnp.int32),
        ],
        compiler_params=params(),
        cost_estimate=cost(2 * dp_size * length * length, 8 * length * dp_size),
    )(route.reshape(dp_size, length))


def rows_of(blocks):
    parts = [b[...] for b in blocks]
    if len(parts) == 1 and parts[0].ndim == 3:
        return parts[0].reshape(-1, parts[0].shape[-1])
    return jnp.concatenate(parts, axis=0)


def place_rows(target_ref, data, begin, count):
    row = begin + lax.broadcasted_iota(jnp.int32, (count, target_ref.shape[1]), 0)
    place = jnp.where(target_ref[...] == row, 1.0, 0.0).astype(jnp.bfloat16)
    return jnp.dot(place, data, preferred_element_type=jnp.float32).astype(jnp.bfloat16)


def pack_other_kernel(number, target_ref, *refs):
    outs = refs[-SWAPS:]
    size = outs[0].shape[0]
    half = size * SWAPS
    packed = place_rows(target_ref, rows_of(refs[:number]), half, half)
    for at, out in enumerate(outs):
        out[...] = packed[at * size : (at + 1) * size]


def pack_own_kernel(number, waits, target_ref, *refs):
    got, refs = refs[:SWAPS], refs[SWAPS:]
    blocks, outs = refs[:number], refs[number + waits :]
    size = got[0].shape[0]
    half = size * SWAPS
    capacity = outs[0].shape[0] // 2
    steps = half // capacity
    packed = place_rows(target_ref, rows_of(blocks), 0, half)
    column = 0
    for first in range(0, len(outs), steps):
        wide = outs[first].shape[1]
        for step in range(steps):
            rows = slice(step * capacity, (step + 1) * capacity)
            outs[first + step][:capacity, :] = packed[rows, column : column + wide]
            begin = step * capacity % size
            part = got[step * capacity // size]
            outs[first + step][capacity:, :] = part[begin : begin + capacity, column : column + wide]
        column += wide


def deliver(target, blocks, widths, dp_size, capacity, after, later):
    wide = blocks[0].shape[-1]
    length = target.shape[1]
    half = dp_size // 2 * capacity
    estimate = cost(2 * half * length * wide, 2 * (half + length) * wide)
    other = pl.pallas_call(
        functools.partial(pack_other_kernel, len(blocks)),
        out_shape=[jax.ShapeDtypeStruct((half // SWAPS, wide), jnp.bfloat16)] * SWAPS,
        in_specs=[VMEM] * (1 + len(blocks)) + [ANY] * len(after),
        compiler_params=params(),
        cost_estimate=estimate,
    )(target, *blocks, *after)
    got = [lax.ppermute(part, "dp", [(j, j ^ 1) for j in range(dp_size)]) for part in other]
    outs = pl.pallas_call(
        functools.partial(pack_own_kernel, len(blocks), len(later)),
        out_shape=[
            jax.ShapeDtypeStruct((2 * capacity, part), jnp.bfloat16)
            for part in widths
            for _ in range(dp_size // 2)
        ],
        in_specs=[VMEM] * (1 + SWAPS + len(blocks)) + [ANY] * len(later),
        compiler_params=params(),
        cost_estimate=estimate,
    )(target, *got, *blocks, *later)
    steps = dp_size // 2
    return [
        swap(list(outs[first : first + steps]), "dp", dp_size, 2)
        for first in range(0, len(outs), steps)
    ]


def attend_kernel(
    heads, doc_most, ctx_size, number, waits, with_kv, stacked, *refs
):
    slot_ref, live_ref, doc_ref, col_ref = refs[:4]
    blocks, refs = refs[4 : 4 + number], refs[4 + number + waits :]
    if with_kv:
        outs, kv_ref, acc = refs[:-2], refs[-2], refs[-1]
    else:
        kv_ref, outs, acc = refs[0], refs[1:-1], refs[-1]
    me = lax.axis_index("ctx")
    pack_len = acc.shape[0]
    wide = heads * HEAD_DIM
    scale = HEAD_DIM ** (-0.5) * math.log2(math.e)
    window = min(pack_len, doc_most + BLOCK)
    row = lax.broadcasted_iota(jnp.int32, (BLOCK, pack_len), 0)
    slot = slot_ref[...]
    live = live_ref[...]
    ones = jnp.ones((window, HEAD_DIM), jnp.bfloat16)
    received = jnp.concatenate([b[...] for b in blocks], axis=0)
    for block in range(pack_len // BLOCK):
        begin = block * BLOCK
        rows = pl.ds(begin, BLOCK)
        place = jnp.where(slot == row + begin, 1.0, 0.0).astype(jnp.bfloat16)
        packed = jnp.dot(place, received, preferred_element_type=jnp.float32).astype(jnp.bfloat16)
        if with_kv:
            kv_ref[rows, :] = packed[:, wide:]
        key_start = max(0, begin + BLOCK - window)
        span = begin + BLOCK - key_start
        keys = kv_ref[pl.ds(key_start, span), :HEAD_DIM]
        values = jnp.concatenate([kv_ref[pl.ds(key_start, span), HEAD_DIM:], ones[:span]], axis=1)
        query_pos = begin + lax.broadcasted_iota(jnp.int32, (BLOCK, span), 0)
        key_pos = key_start + lax.broadcasted_iota(jnp.int32, (BLOCK, span), 1)
        docs = jnp.concatenate([col_ref[rows, :]] * (span // HEAD_DIM), axis=1)
        allowed = (docs == doc_ref[:, pl.ds(key_start, span)]) & (key_pos <= query_pos)
        alive = begin + lax.broadcasted_iota(jnp.int32, (BLOCK, HEAD_DIM), 0) < live
        for head in range(heads):
            query = packed[:, head * HEAD_DIM : (head + 1) * HEAD_DIM]
            scores = lax.dot_general(
                query, keys, (((1,), (1,)), ((), ())), preferred_element_type=jnp.float32
            )
            masked = jnp.where(allowed, scores, -1e30)
            top = jnp.max(masked, axis=1, keepdims=True)
            weights = jnp.exp2((masked - top) * scale).astype(jnp.bfloat16)
            mixed = jnp.dot(weights, values, preferred_element_type=jnp.float32)
            result = mixed[:, :HEAD_DIM] / mixed[:, HEAD_DIM:]
            acc[rows, head * HEAD_DIM : (head + 1) * HEAD_DIM] = jnp.where(
                alive, result, 0.0
            ).astype(jnp.bfloat16)
    part = pack_len // ctx_size
    if stacked:
        outs[0][...] = acc[...].reshape(ctx_size, part, wide)
        return
    for step in range(ctx_size):
        first = pl.multiple_of((me ^ step) * part, part)
        outs[step][...] = acc[pl.ds(first, part), :]


def attend(received, slot, live, doc_row, doc_col, kv, heads, ctx_size, stacked, after):
    pack_len = slot.shape[1]
    doc_most = pack_len // 3
    wide = heads * HEAD_DIM
    with_kv = kv is None
    part = pack_len // ctx_size
    if stacked:
        shapes = [jax.ShapeDtypeStruct((ctx_size, part, wide), jnp.bfloat16)]
    else:
        shapes = [jax.ShapeDtypeStruct((part, wide), jnp.bfloat16)] * ctx_size
    sent = len(shapes)
    if with_kv:
        shapes = shapes + [jax.ShapeDtypeStruct((pack_len, 2 * HEAD_DIM), jnp.bfloat16)]
    work = pack_len * (doc_most + BLOCK) * heads
    outs = pl.pallas_call(
        functools.partial(
            attend_kernel,
            heads,
            doc_most,
            ctx_size,
            len(received),
            len(after),
            with_kv,
            stacked,
        ),
        out_shape=shapes,
        in_specs=[VMEM] * (4 + len(received)) + [ANY] * len(after) + [VMEM] * (0 if with_kv else 1),
        scratch_shapes=[pltpu.VMEM((pack_len, wide), jnp.bfloat16)],
        compiler_params=params(),
        cost_estimate=cost(
            2 * pack_len * pack_len * received[0].shape[1] + 6 * work * HEAD_DIM,
            8 * pack_len * wide,
            work,
        ),
    )(slot, live, doc_row, doc_col, *received, *after, *([] if with_kv else [kv]))
    return list(outs[:sent]), (outs[sent] if with_kv else kv)


def join_kernel(chunk, ctx_size, number, *refs):
    offset, heads = chunk
    heads_dev = Q_HEADS // ctx_size
    blocks = refs[:number]
    out, sem = refs[-2:]
    me = lax.axis_index("ctx")
    copies = []
    for step in range(ctx_size):
        source = step if number == 1 else me ^ step
        block = blocks[0].at[step] if number == 1 else blocks[step]
        column = pl.multiple_of((source * heads_dev + offset) * HEAD_DIM, HEAD_DIM)
        copies.append(
            pltpu.make_async_copy(
                block, out.at[:, pl.ds(column, heads * HEAD_DIM)], sem.at[step]
            )
        )
    for copy in copies:
        copy.start()
    for copy in copies:
        copy.wait()


def join(blocks, chunk, out, ctx_size):
    rows = blocks[0].shape[-2]
    given = [] if out is None else [out]
    number = len(blocks)
    return pl.pallas_call(
        functools.partial(join_kernel, chunk, ctx_size, number),
        out_shape=jax.ShapeDtypeStruct((rows, Q_HEADS * HEAD_DIM), jnp.bfloat16),
        in_specs=[ANY] * (number + len(given)),
        out_specs=ANY,
        scratch_shapes=[pltpu.SemaphoreType.DMA((ctx_size,))],
        input_output_aliases={number: 0} if given else {},
        compiler_params=params(),
        cost_estimate=cost(0, 4 * rows * chunk[1] * HEAD_DIM * ctx_size),
    )(*blocks, *given)


def on_device(q_src, kv_src, route, doc_ids):
    ctx_size = lax.axis_size("ctx")
    dp_size = lax.axis_size("dp")
    length = q_src.shape[0] * ctx_size
    capacity = 3 * length // (2 * dp_size)
    pack_len = dp_size * capacity
    pieces = head_chunks(Q_HEADS // ctx_size)

    gathered, after = [], []
    for at, piece in enumerate(pieces):
        limit = VMEM_LIMIT if at else CUT_LIMIT
        blocks = cut(q_src, kv_src, piece, ctx_size, at == 0, at in STACK_IN, after, limit)
        gathered.append(exchange(blocks, ctx_size))
        after = (gathered[-1] * 2)[1:2] if D1 else blocks[:1]
    target, swapped, slot, live = plan(route, dp_size, ctx_size, capacity)
    doc_col = jnp.broadcast_to(doc_ids.reshape(pack_len, 1), (pack_len, HEAD_DIM))

    received, after = [], []
    for at, blocks in enumerate(gathered):
        widths = [chunk[1] * HEAD_DIM for chunk in pieces[at]]
        widths[0] += 0 if at else 2 * HEAD_DIM
        first = (gathered[at + 1] * 2)[1:2] if PIN_OTHER and at + 1 < len(gathered) else []
        received.append(deliver(target if at in STACK_IN else swapped, blocks, widths, dp_size, capacity, after + first, []))
        after = [received[-1][0][i] for i in PIN_PACK]

    kv, out, sends = None, None, []
    chunks = [chunk for piece in pieces for chunk in piece]
    packed = [blocks for piece in received for blocks in piece]
    for at, chunk in enumerate(chunks):
        after = [packed[i][0] for i in D3 if at == 0 and i < len(packed)]
        if at:
            after = after + kept[:1]
            after = after + [sends[at - 1][i % len(sends[at - 1])] for i in PIN_SENT]
        if at > 1:
            after = after + [sends[at - 2][i % len(sends[at - 2])] for i in PIN_OLD]
        kept, kv = attend(
            packed[at], slot, live, doc_ids, doc_col, kv, chunk[1], ctx_size, at in STACK_OUT, after
        )
        sends.append(exchange(kept, ctx_size))
    for chunk, blocks in zip(chunks, sends):
        out = join(blocks, chunk, out, ctx_size)
    return out


def solution(mesh):
    in_specs = (P(("dp", "ctx"), None), P(("dp", "ctx"), None), P(), P("dp", None))
    out_specs = P(("dp", "ctx"), None)
    return jax.shard_map(
        on_device, mesh=mesh, in_specs=in_specs, out_specs=out_specs, check_vma=False
    )
```

```python
import functools
import math

import jax
import jax.numpy as jnp
from jax import lax
from jax.experimental import pallas as pl
from jax.experimental.pallas import tpu as pltpu
from jax.sharding import PartitionSpec as P

Q_HEADS = 32
KV_HEADS = 4
HEAD_DIM = 128
BLOCK = 128
VMEM_LIMIT = 40 * 1024 * 1024
SHARES = [[4], [4]]
SWAPS = 2
D1 = 0
PIN_OTHER = (1,)
PIN_PACK = (0,)
D3 = (1,)
PIN_SENT = ()
PIN_OLD = ()
PAIRED = ()
ORDER_Z = ()
ORDER_D = ()
ORDER_AT = (0, 1)
ORDER_J = (2, 3, 1, 0)
PIN_HAND = (0,)
HANDS = 2
STACK_OUT = ()
CUT_LIMIT = VMEM_LIMIT
ANY = pl.BlockSpec(memory_space=pl.ANY)
HBM = pl.BlockSpec(memory_space=pltpu.HBM)
VMEM = pl.BlockSpec(memory_space=pltpu.VMEM)


def params(limit=VMEM_LIMIT):
    return pltpu.CompilerParams(vmem_limit_bytes=limit)


def cost(flops, moved, exps=0):
    return pl.CostEstimate(flops=int(flops), bytes_accessed=int(moved), transcendentals=int(exps))


def head_chunks(heads_dev):
    pieces, start = [], 0
    for piece in SHARES:
        chunks = []
        for share in piece:
            size = min(max(1, share * heads_dev // 8), heads_dev - start)
            if size:
                chunks.append((start, size))
                start += size
        if chunks:
            pieces.append(chunks)
    return pieces


def cut_kernel(piece, ctx_size, with_kv, paired, waits, q_ref, kv_ref, *refs):
    outs, sem = refs[waits:-1], refs[-1]
    me = lax.axis_index("ctx")
    heads_dev = Q_HEADS // ctx_size
    group = Q_HEADS // KV_HEADS
    copies = []
    for step in list(range(1, ctx_size)) + [0]:
        owner = me ^ step
        rows = q_ref.shape[0]
        out = outs[2].at[pl.ds((step - 2) * rows, rows)] if paired and step >= 2 else outs[step]
        parts = [(q_ref, owner * heads_dev + piece[0][0], sum([chunk[1] for chunk in piece]))]
        if with_kv:
            head = (owner * heads_dev) // group
            first = piece[0][1]
            parts = [
                (q_ref, owner * heads_dev + piece[0][0], first),
                (kv_ref, head, 1),
                (kv_ref, KV_HEADS + head, 1),
                (q_ref, owner * heads_dev + piece[0][0] + first, parts[0][2] - first),
            ]
        place = 0
        for source, block, number in parts:
            if number:
                wide = number * HEAD_DIM
                column = pl.multiple_of(block * HEAD_DIM, HEAD_DIM)
                copies.append(
                    (source.at[:, pl.ds(column, wide)], out.at[:, pl.ds(place, wide)])
                )
                place += wide
    started = [pltpu.make_async_copy(a, b, sem.at[i]) for i, (a, b) in enumerate(copies)]
    for copy in started:
        copy.start()
    for copy in started:
        copy.wait()


def cut(q_src, kv_src, piece, ctx_size, with_kv, paired, after, limit):
    rows = q_src.shape[0]
    wide = (sum([chunk[1] for chunk in piece]) + (2 if with_kv else 0)) * HEAD_DIM
    shapes = [jax.ShapeDtypeStruct((rows, wide), jnp.bfloat16)] * ctx_size
    if paired:
        shapes = shapes[:2] + [jax.ShapeDtypeStruct((2 * rows, wide), jnp.bfloat16)]
    number = ctx_size * ((4 if len(piece) > 1 else 3) if with_kv else 1)
    outs = pl.pallas_call(
        functools.partial(cut_kernel, piece, ctx_size, with_kv, paired, len(after)),
        out_shape=shapes,
        in_specs=[ANY] * (2 + len(after)),
        out_specs=[VMEM] * len(shapes),
        scratch_shapes=[pltpu.SemaphoreType.DMA((number,))],
        compiler_params=params(limit),
        cost_estimate=cost(0, 4 * ctx_size * rows * wide),
    )(q_src, kv_src, *after)
    return list(outs)


def swap(blocks, axis, size, unit=1):
    return [blocks[0]] + [
        lax.ppermute(blocks[step], axis, [(j, j ^ (step * unit)) for j in range(size)])
        for step in range(1, len(blocks))
    ]


def exchange(blocks, ctx_size):
    if len(blocks) == 1:
        return [lax.all_to_all(blocks[0], "ctx", split_axis=0, concat_axis=0, tiled=True)]
    return swap(blocks, "ctx", ctx_size)


def in_pairs(blocks, ctx_size):
    own, near, far = blocks
    near = lax.ppermute(near, "ctx", [(j, j ^ 1) for j in range(ctx_size)])
    far = lax.ppermute(far, "ctx", [(j, j ^ 2) for j in range(ctx_size)])
    return [own, near, far]


def hand_on_kernel(far_ref, *refs):
    outs = refs[-HANDS:]
    rows = outs[0].shape[0]
    for at, out in enumerate(outs):
        begin = far_ref.shape[0] // 2 + at * rows
        out[...] = far_ref[begin : begin + rows, :]


def hand_on(far, after, ctx_size):
    rows, wide = far.shape[0] // 2, far.shape[1]
    blocks = pl.pallas_call(
        hand_on_kernel,
        out_shape=[jax.ShapeDtypeStruct((rows // HANDS, wide), jnp.bfloat16)] * HANDS,
        in_specs=[VMEM] + [ANY] * len(after),
        compiler_params=params(),
        cost_estimate=cost(0, 4 * rows * wide),
    )(far, *after)
    return [lax.ppermute(b, "ctx", [(j, j ^ 1) for j in range(ctx_size)]) for b in blocks]


def plan_kernel(capacity, ctx_size, route_ref, target_ref, swapped_ref, slot_ref, live_ref):
    dp_size, length = route_ref.shape
    rows = length // ctx_size
    pack_len = dp_size * capacity
    own, me = lax.axis_index("dp"), lax.axis_index("ctx")
    mine = route_ref[pl.ds(own, 1), :]
    seq = lax.broadcasted_iota(jnp.int32, (dp_size, length), 0)
    onehot = jnp.where(mine == seq, 1.0, 0.0)
    earlier = lax.broadcasted_iota(jnp.int32, (length, length), 0)
    later = lax.broadcasted_iota(jnp.int32, (length, length), 1)
    strict = jnp.where(earlier < later, 1.0, 0.0).astype(jnp.bfloat16)
    before = jnp.dot(onehot.astype(jnp.bfloat16), strict, preferred_element_type=jnp.float32)
    rank = jnp.sum(before * onehot, axis=0, keepdims=True).astype(jnp.int32)
    other = mine ^ own
    place = (other & 1) * (dp_size // 2) + (other >> 1)
    target_ref[...] = place * capacity + rank
    for step in range(ctx_size):
        source = me ^ step
        swapped_ref[:, pl.ds(step * rows, rows)] = target_ref[
            :, pl.ds(pl.multiple_of(source * rows, rows), rows)
        ]
    incoming = jnp.sum(
        jnp.where(route_ref[...] == own, 1.0, 0.0), axis=1, keepdims=True
    )
    group = lax.broadcasted_iota(jnp.int32, (dp_size, pack_len), 0)
    lane = lax.broadcasted_iota(jnp.int32, (dp_size, pack_len), 1)
    block = lax.div(lane, capacity)
    source = block ^ own
    start = jnp.sum(jnp.where(group < source, incoming, 0.0), axis=0, keepdims=True)
    amount = jnp.sum(jnp.where(group == source, incoming, 0.0), axis=0, keepdims=True)
    offset = (lane - block * capacity)[:1]
    slot_ref[...] = jnp.where(
        offset < amount.astype(jnp.int32), start.astype(jnp.int32) + offset, -1
    )
    live = jnp.sum(incoming, axis=0, keepdims=True).astype(jnp.int32)
    live_ref[...] = jnp.broadcast_to(live, live_ref.shape)


def plan(route, dp_size, ctx_size, capacity):
    length = route.shape[0] // dp_size
    return pl.pallas_call(
        functools.partial(plan_kernel, capacity, ctx_size),
        out_shape=[
            jax.ShapeDtypeStruct((1, length), jnp.int32),
            jax.ShapeDtypeStruct((1, length), jnp.int32),
            jax.ShapeDtypeStruct((1, dp_size * capacity), jnp.int32),
            jax.ShapeDtypeStruct((1, HEAD_DIM), jnp.int32),
        ],
        compiler_params=params(),
        cost_estimate=cost(2 * dp_size * length * length, 8 * length * dp_size),
    )(route.reshape(dp_size, length))


def mixed_up(blocks, order):
    return [blocks[at] for at in order] if len(order) == len(blocks) else list(blocks)


def restored(refs, order):
    return [refs[order.index(at)] for at in range(len(refs))] if len(order) == len(refs) else refs


def rows_of(blocks):
    rows = blocks[0].shape[0]
    return jnp.concatenate([b[: min(rows, b.shape[0]), :] for b in blocks], axis=0)


def place_rows(target_ref, data, begin, count):
    row = begin + lax.broadcasted_iota(jnp.int32, (count, target_ref.shape[1]), 0)
    place = jnp.where(target_ref[...] == row, 1.0, 0.0).astype(jnp.bfloat16)
    return jnp.dot(place, data, preferred_element_type=jnp.float32).astype(jnp.bfloat16)


def pack_other_kernel(number, order, target_ref, *refs):
    outs = refs[-SWAPS:]
    size = outs[0].shape[0]
    half = size * SWAPS
    packed = place_rows(target_ref, rows_of(restored(refs[:number], order)), half, half)
    for at, out in enumerate(outs):
        out[...] = packed[at * size : (at + 1) * size]


def pack_own_kernel(number, order, waits, target_ref, *refs):
    got, refs = refs[:SWAPS], refs[SWAPS:]
    blocks, outs = refs[:number], refs[number + waits :]
    size = got[0].shape[0]
    half = size * SWAPS
    capacity = outs[0].shape[0] // 2
    steps = half // capacity
    packed = place_rows(target_ref, rows_of(restored(blocks, order)), 0, half)
    column = 0
    for first in range(0, len(outs), steps):
        wide = outs[first].shape[1]
        for step in range(steps):
            rows = slice(step * capacity, (step + 1) * capacity)
            outs[first + step][:capacity, :] = packed[rows, column : column + wide]
            begin = step * capacity % size
            part = got[step * capacity // size]
            outs[first + step][capacity:, :] = part[begin : begin + capacity, column : column + wide]
        column += wide


def deliver(target, blocks, widths, dp_size, capacity, order, after, later):
    wide = blocks[0].shape[-1]
    length = target.shape[1]
    half = dp_size // 2 * capacity
    estimate = cost(2 * half * length * wide, 2 * (half + length) * wide)
    other = pl.pallas_call(
        functools.partial(pack_other_kernel, len(blocks), order),
        out_shape=[jax.ShapeDtypeStruct((half // SWAPS, wide), jnp.bfloat16)] * SWAPS,
        in_specs=[VMEM] * (1 + len(blocks)) + [ANY] * len(after),
        compiler_params=params(),
        cost_estimate=estimate,
    )(target, *mixed_up(blocks, order), *after)
    got = [lax.ppermute(part, "dp", [(j, j ^ 1) for j in range(dp_size)]) for part in other]
    outs = pl.pallas_call(
        functools.partial(pack_own_kernel, len(blocks), order, len(later)),
        out_shape=[
            jax.ShapeDtypeStruct((2 * capacity, part), jnp.bfloat16)
            for part in widths
            for _ in range(dp_size // 2)
        ],
        in_specs=[VMEM] * (1 + SWAPS + len(blocks)) + [ANY] * len(later),
        compiler_params=params(),
        cost_estimate=estimate,
    )(target, *got, *mixed_up(blocks, order), *later)
    steps = dp_size // 2
    return [
        swap(list(outs[first : first + steps]), "dp", dp_size, 2)
        for first in range(0, len(outs), steps)
    ]


def attend_kernel(
    heads, doc_most, ctx_size, number, waits, with_kv, stacked, *refs
):
    slot_ref, live_ref, doc_ref, col_ref = refs[:4]
    blocks, refs = refs[4 : 4 + number], refs[4 + number + waits :]
    if with_kv:
        outs, kv_ref, acc = refs[:-2], refs[-2], refs[-1]
    else:
        kv_ref, outs, acc = refs[0], refs[1:-1], refs[-1]
    me = lax.axis_index("ctx")
    pack_len = acc.shape[0]
    wide = heads * HEAD_DIM
    scale = HEAD_DIM ** (-0.5) * math.log2(math.e)
    window = min(pack_len, doc_most + BLOCK)
    row = lax.broadcasted_iota(jnp.int32, (BLOCK, pack_len), 0)
    slot = slot_ref[...]
    live = live_ref[...]
    ones = jnp.ones((window, HEAD_DIM), jnp.bfloat16)
    received = jnp.concatenate([b[...] for b in restored(blocks, ORDER_D)], axis=0)
    for block in range(pack_len // BLOCK):
        begin = block * BLOCK
        rows = pl.ds(begin, BLOCK)
        place = jnp.where(slot == row + begin, 1.0, 0.0).astype(jnp.bfloat16)
        packed = jnp.dot(place, received, preferred_element_type=jnp.float32).astype(jnp.bfloat16)
        if with_kv:
            kv_ref[rows, :] = packed[:, wide:]
        key_start = max(0, begin + BLOCK - window)
        span = begin + BLOCK - key_start
        keys = kv_ref[pl.ds(key_start, span), :HEAD_DIM]
        values = jnp.concatenate([kv_ref[pl.ds(key_start, span), HEAD_DIM:], ones[:span]], axis=1)
        query_pos = begin + lax.broadcasted_iota(jnp.int32, (BLOCK, span), 0)
        key_pos = key_start + lax.broadcasted_iota(jnp.int32, (BLOCK, span), 1)
        docs = jnp.concatenate([col_ref[rows, :]] * (span // HEAD_DIM), axis=1)
        allowed = (docs == doc_ref[:, pl.ds(key_start, span)]) & (key_pos <= query_pos)
        bias = jnp.where(allowed, 0.0, -1e30)
        alive = begin + lax.broadcasted_iota(jnp.int32, (BLOCK, HEAD_DIM), 0) < live
        queries = jnp.concatenate(
            [packed[:, i * HEAD_DIM : (i + 1) * HEAD_DIM] for i in range(heads)], axis=0
        )
        scores = lax.dot_general(
            queries, keys, (((1,), (1,)), ((), ())), preferred_element_type=jnp.float32
        )
        masked = scores.reshape(heads, BLOCK, span) + bias[None]
        top = jnp.max(masked, axis=2, keepdims=True)
        weights = jnp.exp2((masked - top) * scale).astype(jnp.bfloat16)
        mixed = jnp.dot(
            weights.reshape(heads * BLOCK, span), values, preferred_element_type=jnp.float32
        )
        result = mixed[:, :HEAD_DIM] / mixed[:, HEAD_DIM:]
        for i in range(heads):
            head = jnp.where(alive, result[i * BLOCK : (i + 1) * BLOCK], 0.0)
            acc[rows, i * HEAD_DIM : (i + 1) * HEAD_DIM] = head.astype(jnp.bfloat16)
    part = pack_len // ctx_size
    if stacked:
        outs[0][...] = acc[...].reshape(ctx_size, part, wide)
        return
    for step in range(ctx_size):
        first = pl.multiple_of((me ^ step) * part, part)
        outs[step][...] = acc[pl.ds(first, part), :]


def attend(received, slot, live, doc_row, doc_col, kv, heads, ctx_size, stacked, after):
    pack_len = slot.shape[1]
    doc_most = pack_len // 3
    wide = heads * HEAD_DIM
    with_kv = kv is None
    part = pack_len // ctx_size
    if stacked:
        shapes = [jax.ShapeDtypeStruct((ctx_size, part, wide), jnp.bfloat16)]
    else:
        shapes = [jax.ShapeDtypeStruct((part, wide), jnp.bfloat16)] * ctx_size
    sent = len(shapes)
    if with_kv:
        shapes = shapes + [jax.ShapeDtypeStruct((pack_len, 2 * HEAD_DIM), jnp.bfloat16)]
    work = pack_len * (doc_most + BLOCK) * heads
    outs = pl.pallas_call(
        functools.partial(
            attend_kernel,
            heads,
            doc_most,
            ctx_size,
            len(received),
            len(after),
            with_kv,
            stacked,
        ),
        out_shape=shapes,
        in_specs=[VMEM] * (4 + len(received)) + [ANY] * len(after) + [VMEM] * (0 if with_kv else 1),
        scratch_shapes=[pltpu.VMEM((pack_len, wide), jnp.bfloat16)],
        compiler_params=params(),
        cost_estimate=cost(
            2 * pack_len * pack_len * received[0].shape[1] + 6 * work * HEAD_DIM,
            8 * pack_len * wide,
            work,
        ),
    )(slot, live, doc_row, doc_col, *mixed_up(received, ORDER_D), *after, *([] if with_kv else [kv]))
    return list(outs[:sent]), (outs[sent] if with_kv else kv)


def join_kernel(chunk, ctx_size, number, *refs):
    offset, heads = chunk
    heads_dev = Q_HEADS // ctx_size
    blocks = restored(refs[:number], ORDER_J)
    out, sem = refs[-2:]
    me = lax.axis_index("ctx")
    copies = []
    for step in range(ctx_size):
        source = step if number == 1 else me ^ step
        block = blocks[0].at[step] if number == 1 else blocks[step]
        column = pl.multiple_of((source * heads_dev + offset) * HEAD_DIM, HEAD_DIM)
        copies.append(
            pltpu.make_async_copy(
                block, out.at[:, pl.ds(column, heads * HEAD_DIM)], sem.at[step]
            )
        )
    for copy in copies:
        copy.start()
    for copy in copies:
        copy.wait()


def join(blocks, chunk, out, ctx_size):
    rows = blocks[0].shape[-2]
    given = [] if out is None else [out]
    number = len(blocks)
    return pl.pallas_call(
        functools.partial(join_kernel, chunk, ctx_size, number),
        out_shape=jax.ShapeDtypeStruct((rows, Q_HEADS * HEAD_DIM), jnp.bfloat16),
        in_specs=[ANY] * (number + len(given)),
        out_specs=ANY,
        scratch_shapes=[pltpu.SemaphoreType.DMA((ctx_size,))],
        input_output_aliases={number: 0} if given else {},
        compiler_params=params(),
        cost_estimate=cost(0, 4 * rows * chunk[1] * HEAD_DIM * ctx_size),
    )(*mixed_up(blocks, ORDER_J), *given)


def on_device(q_src, kv_src, route, doc_ids):
    ctx_size = lax.axis_size("ctx")
    dp_size = lax.axis_size("dp")
    length = q_src.shape[0] * ctx_size
    capacity = 3 * length // (2 * dp_size)
    pack_len = dp_size * capacity
    pieces = head_chunks(Q_HEADS // ctx_size)

    target, swapped, slot, live = plan(route, dp_size, ctx_size, capacity)
    doc_col = jnp.broadcast_to(doc_ids.reshape(pack_len, 1), (pack_len, HEAD_DIM))
    gathered, received = [], []

    def bring(at, after):
        limit = VMEM_LIMIT if at else CUT_LIMIT
        paired = at in PAIRED and ctx_size == 4
        blocks = cut(q_src, kv_src, pieces[at], ctx_size, at == 0, paired, after, limit)
        gathered.append(in_pairs(blocks, ctx_size) if paired else exchange(blocks, ctx_size))
        return blocks

    def route_on(at, after):
        widths = [chunk[1] * HEAD_DIM for chunk in pieces[at]]
        widths[0] += 0 if at else 2 * HEAD_DIM
        received.append(deliver(swapped, gathered[at], widths, dp_size, capacity, ORDER_Z if at in ORDER_AT else (), after, []))

    first = bring(0, [])
    if len(pieces) == 1:
        route_on(0, [])
    elif D1 == 2:
        route_on(0, [])
        bring(1, received[0][0][:1])
        route_on(1, [received[0][0][i] for i in PIN_PACK])
    else:
        bring(1, (gathered[0] * 2)[1:2] if D1 else first[:1])
        route_on(0, [gathered[1][i % len(gathered[1])] for i in PIN_OTHER])
        if len(gathered[1]) < ctx_size:
            gathered[1] += hand_on(gathered[1][2], [received[0][0][i] for i in PIN_HAND], ctx_size)
        route_on(1, [received[0][0][i] for i in PIN_PACK])

    kv, out, sends = None, None, []
    chunks = [chunk for piece in pieces for chunk in piece]
    packed = [blocks for piece in received for blocks in piece]
    for at, chunk in enumerate(chunks):
        after = [packed[i][0] for i in D3 if at == 0 and i < len(packed)]
        if at:
            after = after + kept[:1]
            after = after + [sends[at - 1][i % len(sends[at - 1])] for i in PIN_SENT]
        if at > 1:
            after = after + [sends[at - 2][i % len(sends[at - 2])] for i in PIN_OLD]
        kept, kv = attend(
            packed[at], slot, live, doc_ids, doc_col, kv, chunk[1], ctx_size, at in STACK_OUT, after
        )
        sends.append(exchange(kept, ctx_size))
    for chunk, blocks in zip(chunks, sends):
        out = join(blocks, chunk, out, ctx_size)
    return out


def solution(mesh):
    in_specs = (P(("dp", "ctx"), None), P(("dp", "ctx"), None), P(), P("dp", None))
    out_specs = P(("dp", "ctx"), None)
    return jax.shard_map(
        on_device, mesh=mesh, in_specs=in_specs, out_specs=out_specs, check_vma=False
    )
```

```python
import functools
import math

import jax
import jax.numpy as jnp
from jax import lax
from jax.experimental import pallas as pl
from jax.experimental.pallas import tpu as pltpu
from jax.sharding import PartitionSpec as P

Q_HEADS = 32
KV_HEADS = 4
HEAD_DIM = 128
BLOCK = 128
VMEM_LIMIT = 40 * 1024 * 1024
SWAPS = 2
JOIN_ORDER = (2, 3, 1, 0)
ANY = pl.BlockSpec(memory_space=pl.ANY)
VMEM = pl.BlockSpec(memory_space=pltpu.VMEM)


def params():
    return pltpu.CompilerParams(vmem_limit_bytes=VMEM_LIMIT)


def cost(flops, moved, exps=0):
    return pl.CostEstimate(flops=int(flops), bytes_accessed=int(moved), transcendentals=int(exps))


def head_chunks(heads_dev):
    first = max(1, heads_dev // 2)
    return [(0, first)] + ([(first, heads_dev - first)] if heads_dev > first else [])


def cut_kernel(chunk, ctx_size, with_kv, waits, q_ref, kv_ref, *refs):
    offset, heads = chunk
    outs, sem = refs[waits:-1], refs[-1]
    me = lax.axis_index("ctx")
    heads_dev = Q_HEADS // ctx_size
    group = Q_HEADS // KV_HEADS
    copies = []
    for step in list(range(1, ctx_size)) + [0]:
        owner = me ^ step
        parts = [(q_ref, owner * heads_dev + offset, heads)]
        if with_kv:
            head = (owner * heads_dev) // group
            parts += [(kv_ref, head, 1), (kv_ref, KV_HEADS + head, 1)]
        place = 0
        for source, block, number in parts:
            wide = number * HEAD_DIM
            column = pl.multiple_of(block * HEAD_DIM, HEAD_DIM)
            copies.append(
                (source.at[:, pl.ds(column, wide)], outs[step].at[:, pl.ds(place, wide)])
            )
            place += wide
    started = [pltpu.make_async_copy(a, b, sem.at[i]) for i, (a, b) in enumerate(copies)]
    for copy in started:
        copy.start()
    for copy in started:
        copy.wait()


def cut(q_src, kv_src, chunk, ctx_size, with_kv, after):
    rows = q_src.shape[0]
    wide = (chunk[1] + (2 if with_kv else 0)) * HEAD_DIM
    shapes = [jax.ShapeDtypeStruct((rows, wide), jnp.bfloat16)] * ctx_size
    outs = pl.pallas_call(
        functools.partial(cut_kernel, chunk, ctx_size, with_kv, len(after)),
        out_shape=shapes,
        in_specs=[ANY] * (2 + len(after)),
        out_specs=[VMEM] * len(shapes),
        scratch_shapes=[pltpu.SemaphoreType.DMA((ctx_size * (3 if with_kv else 1),))],
        compiler_params=params(),
        cost_estimate=cost(0, 4 * ctx_size * rows * wide),
    )(q_src, kv_src, *after)
    return list(outs)


def swap(blocks, axis, size, unit=1):
    return [blocks[0]] + [
        lax.ppermute(blocks[step], axis, [(j, j ^ (step * unit)) for j in range(size)])
        for step in range(1, len(blocks))
    ]


def plan_kernel(capacity, ctx_size, route_ref, target_ref, slot_ref, live_ref, natural):
    dp_size, length = route_ref.shape
    rows = length // ctx_size
    pack_len = dp_size * capacity
    own, me = lax.axis_index("dp"), lax.axis_index("ctx")
    mine = route_ref[pl.ds(own, 1), :]
    seq = lax.broadcasted_iota(jnp.int32, (dp_size, length), 0)
    onehot = jnp.where(mine == seq, 1.0, 0.0)
    earlier = lax.broadcasted_iota(jnp.int32, (length, length), 0)
    later = lax.broadcasted_iota(jnp.int32, (length, length), 1)
    strict = jnp.where(earlier < later, 1.0, 0.0).astype(jnp.bfloat16)
    before = jnp.dot(onehot.astype(jnp.bfloat16), strict, preferred_element_type=jnp.float32)
    rank = jnp.sum(before * onehot, axis=0, keepdims=True).astype(jnp.int32)
    other = mine ^ own
    place = (other & 1) * (dp_size // 2) + (other >> 1)
    natural[...] = place * capacity + rank
    for step in range(ctx_size):
        source = me ^ step
        target_ref[:, pl.ds(step * rows, rows)] = natural[
            :, pl.ds(pl.multiple_of(source * rows, rows), rows)
        ]
    incoming = jnp.sum(
        jnp.where(route_ref[...] == own, 1.0, 0.0), axis=1, keepdims=True
    )
    group = lax.broadcasted_iota(jnp.int32, (dp_size, pack_len), 0)
    lane = lax.broadcasted_iota(jnp.int32, (dp_size, pack_len), 1)
    block = lax.div(lane, capacity)
    source = block ^ own
    start = jnp.sum(jnp.where(group < source, incoming, 0.0), axis=0, keepdims=True)
    amount = jnp.sum(jnp.where(group == source, incoming, 0.0), axis=0, keepdims=True)
    offset = (lane - block * capacity)[:1]
    slot_ref[...] = jnp.where(
        offset < amount.astype(jnp.int32), start.astype(jnp.int32) + offset, -1
    )
    live = jnp.sum(incoming, axis=0, keepdims=True).astype(jnp.int32)
    live_ref[...] = jnp.broadcast_to(live, live_ref.shape)


def plan(route, dp_size, ctx_size, capacity):
    length = route.shape[0] // dp_size
    return pl.pallas_call(
        functools.partial(plan_kernel, capacity, ctx_size),
        out_shape=[
            jax.ShapeDtypeStruct((1, length), jnp.int32),
            jax.ShapeDtypeStruct((1, dp_size * capacity), jnp.int32),
            jax.ShapeDtypeStruct((1, HEAD_DIM), jnp.int32),
        ],
        scratch_shapes=[pltpu.VMEM((1, length), jnp.int32)],
        compiler_params=params(),
        cost_estimate=cost(2 * dp_size * length * length, 8 * length * dp_size),
    )(route.reshape(dp_size, length))


def rows_of(blocks):
    return jnp.concatenate([b[...] for b in blocks], axis=0)


def place_rows(target_ref, data, begin, count):
    row = begin + lax.broadcasted_iota(jnp.int32, (count, target_ref.shape[1]), 0)
    place = jnp.where(target_ref[...] == row, 1.0, 0.0).astype(jnp.bfloat16)
    return jnp.dot(place, data, preferred_element_type=jnp.float32).astype(jnp.bfloat16)


def pack_other_kernel(number, target_ref, *refs):
    outs = refs[-SWAPS:]
    size = outs[0].shape[0]
    half = size * SWAPS
    packed = place_rows(target_ref, rows_of(refs[:number]), half, half)
    for at, out in enumerate(outs):
        out[...] = packed[at * size : (at + 1) * size]


def pack_own_kernel(number, target_ref, *refs):
    got, refs = refs[:SWAPS], refs[SWAPS:]
    blocks, outs = refs[:number], refs[number:]
    size = got[0].shape[0]
    half = size * SWAPS
    capacity = outs[0].shape[0] // 2
    packed = place_rows(target_ref, rows_of(blocks), 0, half)
    for step, out in enumerate(outs):
        first = step * capacity
        out[:capacity, :] = packed[first : first + capacity]
        begin = first % size
        out[capacity:, :] = got[first // size][begin : begin + capacity, :]


def deliver(target, blocks, dp_size, capacity, after):
    wide = blocks[0].shape[-1]
    length = target.shape[1]
    half = dp_size // 2 * capacity
    estimate = cost(2 * half * length * wide, 2 * (half + length) * wide)
    other = pl.pallas_call(
        functools.partial(pack_other_kernel, len(blocks)),
        out_shape=[jax.ShapeDtypeStruct((half // SWAPS, wide), jnp.bfloat16)] * SWAPS,
        in_specs=[VMEM] * (1 + len(blocks)) + [ANY] * len(after),
        compiler_params=params(),
        cost_estimate=estimate,
    )(target, *blocks, *after)
    got = [lax.ppermute(part, "dp", [(j, j ^ 1) for j in range(dp_size)]) for part in other]
    outs = pl.pallas_call(
        functools.partial(pack_own_kernel, len(blocks)),
        out_shape=[jax.ShapeDtypeStruct((2 * capacity, wide), jnp.bfloat16)] * (dp_size // 2),
        compiler_params=params(),
        cost_estimate=estimate,
    )(target, *got, *blocks)
    return swap(list(outs), "dp", dp_size, 2)


def attend_kernel(
    heads, doc_most, ctx_size, number, waits, with_kv, *refs
):
    slot_ref, live_ref, doc_ref, col_ref = refs[:4]
    blocks, refs = refs[4 : 4 + number], refs[4 + number + waits :]
    if with_kv:
        outs, kv_ref, acc = refs[:-2], refs[-2], refs[-1]
    else:
        kv_ref, outs, acc = refs[0], refs[1:-1], refs[-1]
    me = lax.axis_index("ctx")
    pack_len = acc.shape[0]
    wide = heads * HEAD_DIM
    scale = HEAD_DIM ** (-0.5) * math.log2(math.e)
    window = min(pack_len, doc_most + BLOCK)
    live = live_ref[...]
    ones = jnp.ones((window, HEAD_DIM), jnp.bfloat16)
    received = rows_of(blocks)
    most = 6 * BLOCK
    row = lax.broadcasted_iota(jnp.int32, (most, pack_len), 0)
    for begin in range(0, pack_len, most):
        place = jnp.where(slot_ref[...] == row + begin, 1.0, 0.0).astype(jnp.bfloat16)
        packed = jnp.dot(place, received, preferred_element_type=jnp.float32).astype(jnp.bfloat16)
        acc[begin : begin + most, :] = packed[:, :wide]
        if with_kv:
            kv_ref[begin : begin + most, :] = packed[:, wide:]
    for block in range(pack_len // BLOCK):
        begin = block * BLOCK
        rows = pl.ds(begin, BLOCK)
        packed = acc[rows, :]
        key_start = max(0, begin + BLOCK - window)
        span = begin + BLOCK - key_start
        keys = kv_ref[pl.ds(key_start, span), :HEAD_DIM]
        values = jnp.concatenate([kv_ref[pl.ds(key_start, span), HEAD_DIM:], ones[:span]], axis=1)
        query_pos = begin + lax.broadcasted_iota(jnp.int32, (BLOCK, span), 0)
        key_pos = key_start + lax.broadcasted_iota(jnp.int32, (BLOCK, span), 1)
        docs = jnp.concatenate([col_ref[rows, :]] * (span // HEAD_DIM), axis=1)
        allowed = (docs == doc_ref[:, pl.ds(key_start, span)]) & (key_pos <= query_pos)
        bias = jnp.where(allowed, 0.0, -1e30)
        alive = begin + lax.broadcasted_iota(jnp.int32, (BLOCK, HEAD_DIM), 0) < live
        queries = jnp.concatenate(
            [packed[:, i * HEAD_DIM : (i + 1) * HEAD_DIM] for i in range(heads)], axis=0
        )
        scores = lax.dot_general(
            queries, keys, (((1,), (1,)), ((), ())), preferred_element_type=jnp.float32
        )
        masked = scores.reshape(heads, BLOCK, span) + bias[None]
        top = jnp.max(masked, axis=2, keepdims=True)
        weights = jnp.exp2((masked - top) * scale).astype(jnp.bfloat16)
        mixed = jnp.dot(
            weights.reshape(heads * BLOCK, span), values, preferred_element_type=jnp.float32
        )
        result = mixed[:, :HEAD_DIM] / mixed[:, HEAD_DIM:]
        for i in range(heads):
            head = jnp.where(alive, result[i * BLOCK : (i + 1) * BLOCK], 0.0)
            acc[rows, i * HEAD_DIM : (i + 1) * HEAD_DIM] = head.astype(jnp.bfloat16)
    part = pack_len // ctx_size
    for step in range(ctx_size):
        first = pl.multiple_of((me ^ step) * part, part)
        outs[step][...] = acc[pl.ds(first, part), :]


def attend(received, slot, live, doc_row, doc_col, kv, heads, ctx_size, after):
    pack_len = slot.shape[1]
    doc_most = pack_len // 3
    wide = heads * HEAD_DIM
    with_kv = kv is None
    part = pack_len // ctx_size
    shapes = [jax.ShapeDtypeStruct((part, wide), jnp.bfloat16)] * ctx_size
    sent = len(shapes)
    if with_kv:
        shapes = shapes + [jax.ShapeDtypeStruct((pack_len, 2 * HEAD_DIM), jnp.bfloat16)]
    work = pack_len * (doc_most + BLOCK) * heads
    outs = pl.pallas_call(
        functools.partial(
            attend_kernel,
            heads,
            doc_most,
            ctx_size,
            len(received),
            len(after),
            with_kv,
        ),
        out_shape=shapes,
        in_specs=[VMEM] * (4 + len(received)) + [ANY] * len(after) + [VMEM] * (0 if with_kv else 1),
        scratch_shapes=[pltpu.VMEM((pack_len, wide), jnp.bfloat16)],
        compiler_params=params(),
        cost_estimate=cost(
            2 * pack_len * pack_len * received[0].shape[1] + 6 * work * HEAD_DIM,
            8 * pack_len * wide,
            work,
        ),
    )(slot, live, doc_row, doc_col, *received, *after, *([] if with_kv else [kv]))
    return list(outs[:sent]), (outs[sent] if with_kv else kv)


def join_kernel(chunk, ctx_size, steps, *refs):
    offset, heads = chunk
    heads_dev = Q_HEADS // ctx_size
    out, sem = refs[-2:]
    me = lax.axis_index("ctx")
    copies = []
    for at, step in enumerate(steps):
        column = pl.multiple_of(((me ^ step) * heads_dev + offset) * HEAD_DIM, HEAD_DIM)
        copies.append(
            pltpu.make_async_copy(
                refs[at], out.at[:, pl.ds(column, heads * HEAD_DIM)], sem.at[at]
            )
        )
    for copy in copies:
        copy.start()
    for copy in copies:
        copy.wait()


def join(blocks, chunk, out, ctx_size):
    rows = blocks[0].shape[0]
    given = [] if out is None else [out]
    steps = JOIN_ORDER if len(JOIN_ORDER) == ctx_size else tuple(range(ctx_size))
    return pl.pallas_call(
        functools.partial(join_kernel, chunk, ctx_size, steps),
        out_shape=jax.ShapeDtypeStruct((rows, Q_HEADS * HEAD_DIM), jnp.bfloat16),
        in_specs=[ANY] * (ctx_size + len(given)),
        out_specs=ANY,
        scratch_shapes=[pltpu.SemaphoreType.DMA((ctx_size,))],
        input_output_aliases={ctx_size: 0} if given else {},
        compiler_params=params(),
        cost_estimate=cost(0, 4 * rows * chunk[1] * HEAD_DIM * ctx_size),
    )(*[blocks[step] for step in steps], *given)


def on_device(q_src, kv_src, route, doc_ids):
    ctx_size = lax.axis_size("ctx")
    dp_size = lax.axis_size("dp")
    length = q_src.shape[0] * ctx_size
    capacity = 3 * length // (2 * dp_size)
    pack_len = dp_size * capacity
    chunks = head_chunks(Q_HEADS // ctx_size)

    gathered, after = [], []
    for at, chunk in enumerate(chunks):
        blocks = cut(q_src, kv_src, chunk, ctx_size, at == 0, after)
        gathered.append(swap(blocks, "ctx", ctx_size))
        after = blocks[:1]
    target, slot, live = plan(route, dp_size, ctx_size, capacity)
    doc_col = jnp.broadcast_to(doc_ids.reshape(pack_len, 1), (pack_len, HEAD_DIM))

    packed = []
    for at, blocks in enumerate(gathered):
        after = [blocks[1] for blocks in gathered[at + 1 : at + 2]] + [p[0] for p in packed[-1:]]
        packed.append(deliver(target, blocks, dp_size, capacity, after))

    kv, sends = None, []
    for at, chunk in enumerate(chunks):
        after = [sends[-1][0]] if sends else [p[0] for p in packed[1:2]]
        blocks, kv = attend(
            packed[at], slot, live, doc_ids, doc_col, kv, chunk[1], ctx_size, after
        )
        sends.append(swap(blocks, "ctx", ctx_size))
    out = None
    for chunk, blocks in zip(chunks, sends):
        out = join(blocks, chunk, out, ctx_size)
    return out


def solution(mesh):
    in_specs = (P(("dp", "ctx"), None), P(("dp", "ctx"), None), P(), P("dp", None))
    out_specs = P(("dp", "ctx"), None)
    return jax.shard_map(
        on_device, mesh=mesh, in_specs=in_specs, out_specs=out_specs, check_vma=False
    )
```

```python
import functools
import math

import jax
import jax.numpy as jnp
from jax import lax
from jax.experimental import pallas as pl
from jax.experimental.pallas import tpu as pltpu
from jax.sharding import PartitionSpec as P

Q_HEADS = 32
KV_HEADS = 4
HEAD_DIM = 128
BLOCK = 128
VMEM_LIMIT = 40 * 1024 * 1024
SWAPS = 2
JOIN_ORDER = (2, 3, 1, 0)
ANY = pl.BlockSpec(memory_space=pl.ANY)
VMEM = pl.BlockSpec(memory_space=pltpu.VMEM)


def params():
    return pltpu.CompilerParams(vmem_limit_bytes=VMEM_LIMIT)


def cost(flops, moved, exps=0):
    return pl.CostEstimate(flops=int(flops), bytes_accessed=int(moved), transcendentals=int(exps))


def head_chunks(heads_dev):
    first = max(1, heads_dev // 2)
    return [(0, first)] + ([(first, heads_dev - first)] if heads_dev > first else [])


def cut_kernel(chunk, ctx_size, with_kv, waits, q_ref, *refs):
    offset, heads = chunk
    kv_ref, refs = (refs[0], refs[1:]) if with_kv else (None, refs)
    outs, sem = refs[waits:-1], refs[-1]
    me = lax.axis_index("ctx")
    heads_dev = Q_HEADS // ctx_size
    group = Q_HEADS // KV_HEADS
    copies = []
    for step in list(range(1, ctx_size)) + [0]:
        owner = me ^ step
        parts = [(q_ref, owner * heads_dev + offset, heads)]
        if with_kv:
            head = (owner * heads_dev) // group
            parts += [(kv_ref, head, 1), (kv_ref, KV_HEADS + head, 1)]
        place = 0
        for source, block, number in parts:
            wide = number * HEAD_DIM
            column = pl.multiple_of(block * HEAD_DIM, HEAD_DIM)
            copies.append(
                (source.at[:, pl.ds(column, wide)], outs[step].at[:, pl.ds(place, wide)])
            )
            place += wide
    started = [pltpu.make_async_copy(a, b, sem.at[i]) for i, (a, b) in enumerate(copies)]
    for copy in started:
        copy.start()
    for copy in started:
        copy.wait()


def cut(q_src, kv_src, chunk, ctx_size, with_kv, after):
    rows = q_src.shape[0]
    wide = (chunk[1] + (2 if with_kv else 0)) * HEAD_DIM
    shapes = [jax.ShapeDtypeStruct((rows, wide), jnp.bfloat16)] * ctx_size
    sources = [q_src, kv_src] if with_kv else [q_src]
    sources = [pltpu.with_memory_space_constraint(x, pltpu.HBM) for x in sources]
    outs = pl.pallas_call(
        functools.partial(cut_kernel, chunk, ctx_size, with_kv, len(after)),
        out_shape=shapes,
        in_specs=[ANY] * (len(sources) + len(after)),
        out_specs=[VMEM] * len(shapes),
        scratch_shapes=[pltpu.SemaphoreType.DMA((ctx_size * (3 if with_kv else 1),))],
        compiler_params=params(),
        cost_estimate=cost(0, 4 * ctx_size * rows * wide),
    )(*sources, *after)
    return list(outs)


def swap(blocks, axis, size, unit=1):
    return [blocks[0]] + [
        lax.ppermute(blocks[step], axis, [(j, j ^ (step * unit)) for j in range(size)])
        for step in range(1, len(blocks))
    ]


def plan_kernel(capacity, ctx_size, route_ref, target_ref, slot_ref, live_ref, natural):
    dp_size, length = route_ref.shape
    rows = length // ctx_size
    pack_len = dp_size * capacity
    own, me = lax.axis_index("dp"), lax.axis_index("ctx")
    mine = route_ref[pl.ds(own, 1), :]
    seq = lax.broadcasted_iota(jnp.int32, (dp_size, length), 0)
    onehot = jnp.where(mine == seq, 1.0, 0.0)
    earlier = lax.broadcasted_iota(jnp.int32, (length, length), 0)
    later = lax.broadcasted_iota(jnp.int32, (length, length), 1)
    strict = jnp.where(earlier < later, 1.0, 0.0).astype(jnp.bfloat16)
    before = jnp.dot(onehot.astype(jnp.bfloat16), strict, preferred_element_type=jnp.float32)
    rank = jnp.sum(before * onehot, axis=0, keepdims=True).astype(jnp.int32)
    other = mine ^ own
    place = (other & 1) * (dp_size // 2) + (other >> 1)
    natural[...] = place * capacity + rank
    for step in range(ctx_size):
        source = me ^ step
        target_ref[:, pl.ds(step * rows, rows)] = natural[
            :, pl.ds(pl.multiple_of(source * rows, rows), rows)
        ]
    incoming = jnp.sum(
        jnp.where(route_ref[...] == own, 1.0, 0.0), axis=1, keepdims=True
    )
    group = lax.broadcasted_iota(jnp.int32, (dp_size, pack_len), 0)
    lane = lax.broadcasted_iota(jnp.int32, (dp_size, pack_len), 1)
    block = lax.div(lane, capacity)
    source = block ^ own
    start = jnp.sum(jnp.where(group < source, incoming, 0.0), axis=0, keepdims=True)
    amount = jnp.sum(jnp.where(group == source, incoming, 0.0), axis=0, keepdims=True)
    offset = (lane - block * capacity)[:1]
    slot_ref[...] = jnp.where(
        offset < amount.astype(jnp.int32), start.astype(jnp.int32) + offset, -1
    )
    live = jnp.sum(incoming, axis=0, keepdims=True).astype(jnp.int32)
    live_ref[...] = jnp.broadcast_to(live, live_ref.shape)


def plan(route, dp_size, ctx_size, capacity):
    length = route.shape[0] // dp_size
    return pl.pallas_call(
        functools.partial(plan_kernel, capacity, ctx_size),
        out_shape=[
            jax.ShapeDtypeStruct((1, length), jnp.int32),
            jax.ShapeDtypeStruct((1, dp_size * capacity), jnp.int32),
            jax.ShapeDtypeStruct((1, HEAD_DIM), jnp.int32),
        ],
        scratch_shapes=[pltpu.VMEM((1, length), jnp.int32)],
        compiler_params=params(),
        cost_estimate=cost(2 * dp_size * length * length, 8 * length * dp_size),
    )(route.reshape(dp_size, length))


def rows_of(blocks):
    return jnp.concatenate([b[...] for b in blocks], axis=0)


def place_rows(target_ref, data, begin, count):
    row = begin + lax.broadcasted_iota(jnp.int32, (count, target_ref.shape[1]), 0)
    place = jnp.where(target_ref[...] == row, 1.0, 0.0).astype(jnp.bfloat16)
    return jnp.dot(place, data, preferred_element_type=jnp.float32).astype(jnp.bfloat16)


def pack_other_kernel(number, target_ref, *refs):
    outs = refs[-SWAPS:]
    size = outs[0].shape[0]
    half = size * SWAPS
    packed = place_rows(target_ref, rows_of(refs[:number]), half, half)
    for at, out in enumerate(outs):
        out[...] = packed[at * size : (at + 1) * size]


def pack_own_kernel(number, target_ref, *refs):
    got, refs = refs[:SWAPS], refs[SWAPS:]
    blocks, outs = refs[:number], refs[number:]
    size = got[0].shape[0]
    half = size * SWAPS
    capacity = outs[0].shape[0] // 2
    packed = place_rows(target_ref, rows_of(blocks), 0, half)
    for step, out in enumerate(outs):
        first = step * capacity
        out[:capacity, :] = packed[first : first + capacity]
        begin = first % size
        out[capacity:, :] = got[first // size][begin : begin + capacity, :]


def deliver(target, blocks, dp_size, capacity, after):
    wide = blocks[0].shape[-1]
    length = target.shape[1]
    half = dp_size // 2 * capacity
    estimate = cost(2 * half * length * wide, 2 * (half + length) * wide)
    other = pl.pallas_call(
        functools.partial(pack_other_kernel, len(blocks)),
        out_shape=[jax.ShapeDtypeStruct((half // SWAPS, wide), jnp.bfloat16)] * SWAPS,
        in_specs=[VMEM] * (1 + len(blocks)) + [ANY] * len(after),
        compiler_params=params(),
        cost_estimate=estimate,
    )(target, *blocks, *after)
    got = [lax.ppermute(part, "dp", [(j, j ^ 1) for j in range(dp_size)]) for part in other]
    outs = pl.pallas_call(
        functools.partial(pack_own_kernel, len(blocks)),
        out_shape=[jax.ShapeDtypeStruct((2 * capacity, wide), jnp.bfloat16)] * (dp_size // 2),
        compiler_params=params(),
        cost_estimate=estimate,
    )(target, *got, *blocks)
    return swap(list(outs), "dp", dp_size, 2)


def attend_kernel(
    heads, doc_most, ctx_size, number, waits, with_kv, *refs
):
    slot_ref, live_ref, doc_ref, col_ref = refs[:4]
    blocks, refs = refs[4 : 4 + number], refs[4 + number + waits :]
    if with_kv:
        outs, kv_ref, acc = refs[:-2], refs[-2], refs[-1]
    else:
        kv_ref, outs, acc = refs[0], refs[1:-1], refs[-1]
    me = lax.axis_index("ctx")
    pack_len = acc.shape[0]
    wide = heads * HEAD_DIM
    scale = HEAD_DIM ** (-0.5) * math.log2(math.e)
    window = min(pack_len, doc_most + BLOCK)
    live = live_ref[...]
    ones = jnp.ones((window, HEAD_DIM), jnp.bfloat16)
    received = rows_of(blocks)
    most = 6 * BLOCK
    row = lax.broadcasted_iota(jnp.int32, (most, pack_len), 0)
    for begin in range(0, pack_len, most):
        place = jnp.where(slot_ref[...] == row + begin, 1.0, 0.0).astype(jnp.bfloat16)
        packed = jnp.dot(place, received, preferred_element_type=jnp.float32).astype(jnp.bfloat16)
        acc[begin : begin + most, :] = packed[:, :wide]
        if with_kv:
            kv_ref[begin : begin + most, :] = packed[:, wide:]
    for block in range(pack_len // BLOCK):
        begin = block * BLOCK
        rows = pl.ds(begin, BLOCK)
        packed = acc[rows, :]
        key_start = max(0, begin + BLOCK - window)
        span = begin + BLOCK - key_start
        keys = kv_ref[pl.ds(key_start, span), :HEAD_DIM]
        values = jnp.concatenate([kv_ref[pl.ds(key_start, span), HEAD_DIM:], ones[:span]], axis=1)
        query_pos = begin + lax.broadcasted_iota(jnp.int32, (BLOCK, span), 0)
        key_pos = key_start + lax.broadcasted_iota(jnp.int32, (BLOCK, span), 1)
        docs = jnp.concatenate([col_ref[rows, :]] * (span // HEAD_DIM), axis=1)
        allowed = (docs == doc_ref[:, pl.ds(key_start, span)]) & (key_pos <= query_pos)
        bias = jnp.where(allowed, 0.0, -1e30)
        alive = begin + lax.broadcasted_iota(jnp.int32, (BLOCK, HEAD_DIM), 0) < live
        queries = jnp.concatenate(
            [packed[:, i * HEAD_DIM : (i + 1) * HEAD_DIM] for i in range(heads)], axis=0
        )
        scores = lax.dot_general(
            queries, keys, (((1,), (1,)), ((), ())), preferred_element_type=jnp.float32
        )
        masked = scores.reshape(heads, BLOCK, span) + bias[None]
        top = jnp.max(masked, axis=2, keepdims=True)
        weights = jnp.exp2((masked - top) * scale).astype(jnp.bfloat16)
        mixed = jnp.dot(
            weights.reshape(heads * BLOCK, span), values, preferred_element_type=jnp.float32
        )
        result = mixed[:, :HEAD_DIM] / mixed[:, HEAD_DIM:]
        for i in range(heads):
            head = jnp.where(alive, result[i * BLOCK : (i + 1) * BLOCK], 0.0)
            acc[rows, i * HEAD_DIM : (i + 1) * HEAD_DIM] = head.astype(jnp.bfloat16)
    part = pack_len // ctx_size
    for step in range(ctx_size):
        first = pl.multiple_of((me ^ step) * part, part)
        outs[step][...] = acc[pl.ds(first, part), :]


def attend(received, slot, live, doc_row, doc_col, kv, heads, ctx_size, after):
    pack_len = slot.shape[1]
    doc_most = pack_len // 3
    wide = heads * HEAD_DIM
    with_kv = kv is None
    part = pack_len // ctx_size
    shapes = [jax.ShapeDtypeStruct((part, wide), jnp.bfloat16)] * ctx_size
    sent = len(shapes)
    if with_kv:
        shapes = shapes + [jax.ShapeDtypeStruct((pack_len, 2 * HEAD_DIM), jnp.bfloat16)]
    work = pack_len * (doc_most + BLOCK) * heads
    outs = pl.pallas_call(
        functools.partial(
            attend_kernel,
            heads,
            doc_most,
            ctx_size,
            len(received),
            len(after),
            with_kv,
        ),
        out_shape=shapes,
        in_specs=[VMEM] * (4 + len(received)) + [ANY] * len(after) + [VMEM] * (0 if with_kv else 1),
        scratch_shapes=[pltpu.VMEM((pack_len, wide), jnp.bfloat16)],
        compiler_params=params(),
        cost_estimate=cost(
            2 * pack_len * pack_len * received[0].shape[1] + 6 * work * HEAD_DIM,
            8 * pack_len * wide,
            work,
        ),
    )(slot, live, doc_row, doc_col, *received, *after, *([] if with_kv else [kv]))
    return list(outs[:sent]), (outs[sent] if with_kv else kv)


def join_kernel(chunk, ctx_size, steps, *refs):
    offset, heads = chunk
    heads_dev = Q_HEADS // ctx_size
    out, sem = refs[-2:]
    me = lax.axis_index("ctx")
    copies = []
    for at, step in enumerate(steps):
        column = pl.multiple_of(((me ^ step) * heads_dev + offset) * HEAD_DIM, HEAD_DIM)
        copies.append(
            pltpu.make_async_copy(
                refs[at], out.at[:, pl.ds(column, heads * HEAD_DIM)], sem.at[at]
            )
        )
    for copy in copies:
        copy.start()
    for copy in copies:
        copy.wait()


def join(blocks, chunk, out, ctx_size):
    rows = blocks[0].shape[0]
    given = [] if out is None else [out]
    steps = JOIN_ORDER if len(JOIN_ORDER) == ctx_size else tuple(range(ctx_size))
    return pl.pallas_call(
        functools.partial(join_kernel, chunk, ctx_size, steps),
        out_shape=jax.ShapeDtypeStruct((rows, Q_HEADS * HEAD_DIM), jnp.bfloat16),
        in_specs=[ANY] * (ctx_size + len(given)),
        out_specs=ANY,
        scratch_shapes=[pltpu.SemaphoreType.DMA((ctx_size,))],
        input_output_aliases={ctx_size: 0} if given else {},
        compiler_params=params(),
        cost_estimate=cost(0, 4 * rows * chunk[1] * HEAD_DIM * ctx_size),
    )(*[blocks[step] for step in steps], *given)


def on_device(q_src, kv_src, route, doc_ids):
    ctx_size = lax.axis_size("ctx")
    dp_size = lax.axis_size("dp")
    length = q_src.shape[0] * ctx_size
    capacity = 3 * length // (2 * dp_size)
    pack_len = dp_size * capacity
    chunks = head_chunks(Q_HEADS // ctx_size)

    gathered, after = [], []
    for at, chunk in enumerate(chunks):
        blocks = cut(q_src, kv_src, chunk, ctx_size, at == 0, after)
        gathered.append(swap(blocks, "ctx", ctx_size))
        after = blocks[:1]
    target, slot, live = plan(route, dp_size, ctx_size, capacity)
    doc_col = jnp.broadcast_to(doc_ids.reshape(pack_len, 1), (pack_len, HEAD_DIM))

    packed = []
    for at, blocks in enumerate(gathered):
        after = [blocks[1] for blocks in gathered[at + 1 : at + 2]] + [p[0] for p in packed[-1:]]
        packed.append(deliver(target, blocks, dp_size, capacity, after))

    kv, sends = None, []
    for at, chunk in enumerate(chunks):
        after = [sends[-1][0]] if sends else [p[0] for p in packed[1:2]]
        blocks, kv = attend(
            packed[at], slot, live, doc_ids, doc_col, kv, chunk[1], ctx_size, after
        )
        sends.append(swap(blocks, "ctx", ctx_size))
    out = None
    for chunk, blocks in zip(chunks, sends):
        out = join(blocks, chunk, out, ctx_size)
    return out


def solution(mesh):
    in_specs = (P(("dp", "ctx"), None), P(("dp", "ctx"), None), P(), P("dp", None))
    out_specs = P(("dp", "ctx"), None)
    return jax.shard_map(
        on_device, mesh=mesh, in_specs=in_specs, out_specs=out_specs, check_vma=False
    )
```

```python
import functools
import math

import jax
import jax.numpy as jnp
from jax import lax
from jax.experimental import pallas as pl
from jax.experimental.pallas import tpu as pltpu
from jax.sharding import PartitionSpec as P

Q_HEADS = 32
KV_HEADS = 4
HEAD_DIM = 128
BLOCK = 128
VMEM_LIMIT = 40 * 1024 * 1024
SWAPS = 2
JOIN_ORDER = (2, 3, 1, 0)
ANY = pl.BlockSpec(memory_space=pl.ANY)
VMEM = pl.BlockSpec(memory_space=pltpu.VMEM)


def params():
    return pltpu.CompilerParams(vmem_limit_bytes=VMEM_LIMIT)


def cost(flops, moved, exps=0):
    return pl.CostEstimate(flops=int(flops), bytes_accessed=int(moved), transcendentals=int(exps))


def head_chunks(heads_dev):
    first = max(1, heads_dev // 2)
    return [(0, first)] + ([(first, heads_dev - first)] if heads_dev > first else [])


def cut_kernel(chunk, ctx_size, with_kv, waits, q_ref, *refs):
    offset, heads = chunk
    kv_ref, refs = (refs[0], refs[1:]) if with_kv else (None, refs)
    outs, sem = refs[waits:-1], refs[-1]
    me = lax.axis_index("ctx")
    heads_dev = Q_HEADS // ctx_size
    group = Q_HEADS // KV_HEADS
    copies = []
    for step in list(range(1, ctx_size)) + [0]:
        owner = me ^ step
        parts = [(q_ref, owner * heads_dev + offset, heads)]
        if with_kv:
            head = (owner * heads_dev) // group
            parts += [(kv_ref, head, 1), (kv_ref, KV_HEADS + head, 1)]
        place = 0
        for source, block, number in parts:
            wide = number * HEAD_DIM
            column = pl.multiple_of(block * HEAD_DIM, HEAD_DIM)
            copies.append(
                (source.at[:, pl.ds(column, wide)], outs[step].at[:, pl.ds(place, wide)])
            )
            place += wide
    started = [pltpu.make_async_copy(a, b, sem.at[i]) for i, (a, b) in enumerate(copies)]
    for copy in started:
        copy.start()
    for copy in started:
        copy.wait()


def cut(q_src, kv_src, chunk, ctx_size, with_kv, after):
    rows = q_src.shape[0]
    wide = (chunk[1] + (2 if with_kv else 0)) * HEAD_DIM
    shapes = [jax.ShapeDtypeStruct((rows, wide), jnp.bfloat16)] * ctx_size
    sources = [q_src, kv_src] if with_kv else [q_src]
    sources = [pltpu.with_memory_space_constraint(x, pltpu.HBM) for x in sources]
    outs = pl.pallas_call(
        functools.partial(cut_kernel, chunk, ctx_size, with_kv, len(after)),
        out_shape=shapes,
        in_specs=[ANY] * (len(sources) + len(after)),
        out_specs=[VMEM] * len(shapes),
        scratch_shapes=[pltpu.SemaphoreType.DMA((ctx_size * (3 if with_kv else 1),))],
        compiler_params=params(),
        cost_estimate=cost(0, 4 * ctx_size * rows * wide),
    )(*sources, *after)
    return list(outs)


def swap(blocks, axis, size, unit=1):
    return [blocks[0]] + [
        lax.ppermute(blocks[step], axis, [(j, j ^ (step * unit)) for j in range(size)])
        for step in range(1, len(blocks))
    ]


def plan_kernel(capacity, ctx_size, route_ref, _, target_ref, slot_ref, live_ref, natural):
    dp_size, length = route_ref.shape
    rows = length // ctx_size
    pack_len = dp_size * capacity
    own, me = lax.axis_index("dp"), lax.axis_index("ctx")
    mine = route_ref[pl.ds(own, 1), :]
    seq = lax.broadcasted_iota(jnp.int32, (dp_size, length), 0)
    onehot = jnp.where(mine == seq, 1.0, 0.0)
    earlier = lax.broadcasted_iota(jnp.int32, (length, length), 0)
    later = lax.broadcasted_iota(jnp.int32, (length, length), 1)
    strict = jnp.where(earlier < later, 1.0, 0.0).astype(jnp.bfloat16)
    before = jnp.dot(onehot.astype(jnp.bfloat16), strict, preferred_element_type=jnp.float32)
    rank = jnp.sum(before * onehot, axis=0, keepdims=True).astype(jnp.int32)
    other = mine ^ own
    place = (other & 1) * (dp_size // 2) + (other >> 1)
    natural[...] = place * capacity + rank
    for step in range(ctx_size):
        source = me ^ step
        target_ref[:, pl.ds(step * rows, rows)] = natural[
            :, pl.ds(pl.multiple_of(source * rows, rows), rows)
        ]
    incoming = jnp.sum(
        jnp.where(route_ref[...] == own, 1.0, 0.0), axis=1, keepdims=True
    )
    group = lax.broadcasted_iota(jnp.int32, (dp_size, pack_len), 0)
    lane = lax.broadcasted_iota(jnp.int32, (dp_size, pack_len), 1)
    block = lax.div(lane, capacity)
    source = block ^ own
    start = jnp.sum(jnp.where(group < source, incoming, 0.0), axis=0, keepdims=True)
    amount = jnp.sum(jnp.where(group == source, incoming, 0.0), axis=0, keepdims=True)
    offset = (lane - block * capacity)[:1]
    slot_ref[...] = jnp.where(
        offset < amount.astype(jnp.int32), start.astype(jnp.int32) + offset, -1
    )
    live = jnp.sum(incoming, axis=0, keepdims=True).astype(jnp.int32)
    live_ref[...] = jnp.broadcast_to(live, live_ref.shape)


def plan(route, dp_size, ctx_size, capacity, after):
    length = route.shape[0] // dp_size
    return pl.pallas_call(
        functools.partial(plan_kernel, capacity, ctx_size),
        out_shape=[
            jax.ShapeDtypeStruct((1, length), jnp.int32),
            jax.ShapeDtypeStruct((1, dp_size * capacity), jnp.int32),
            jax.ShapeDtypeStruct((1, HEAD_DIM), jnp.int32),
        ],
        in_specs=[VMEM, ANY],
        scratch_shapes=[pltpu.VMEM((1, length), jnp.int32)],
        compiler_params=params(),
        cost_estimate=cost(2 * dp_size * length * length, 8 * length * dp_size),
    )(route.reshape(dp_size, length), after)


def rows_of(blocks):
    return jnp.concatenate([b[...] for b in blocks], axis=0)


def place_rows(target_ref, data, begin, count):
    row = begin + lax.broadcasted_iota(jnp.int32, (count, target_ref.shape[1]), 0)
    place = jnp.where(target_ref[...] == row, 1.0, 0.0).astype(jnp.bfloat16)
    return jnp.dot(place, data, preferred_element_type=jnp.float32).astype(jnp.bfloat16)


def pack_other_kernel(number, target_ref, *refs):
    outs = refs[-SWAPS:]
    size = outs[0].shape[0]
    half = size * SWAPS
    packed = place_rows(target_ref, rows_of(refs[:number]), half, half)
    for at, out in enumerate(outs):
        out[...] = packed[at * size : (at + 1) * size]


def pack_own_kernel(target_ref, *refs):
    refs[-1][...] = place_rows(target_ref, rows_of(refs[:-1]), 0, refs[-1].shape[0])


def merge_kernel(own_ref, *refs):
    got, outs = refs[:SWAPS], refs[SWAPS:]
    size = got[0].shape[0]
    capacity = outs[0].shape[0] // 2
    for step, out in enumerate(outs):
        first = step * capacity
        out[:capacity, :] = own_ref[first : first + capacity, :]
        begin = first % size
        out[capacity:, :] = got[first // size][begin : begin + capacity, :]


def deliver(target, blocks, dp_size, capacity, after):
    wide = blocks[0].shape[-1]
    length = target.shape[1]
    half = dp_size // 2 * capacity
    estimate = cost(2 * half * length * wide, 2 * (half + length) * wide)
    other = pl.pallas_call(
        functools.partial(pack_other_kernel, len(blocks)),
        out_shape=[jax.ShapeDtypeStruct((half // SWAPS, wide), jnp.bfloat16)] * SWAPS,
        in_specs=[VMEM] * (1 + len(blocks)) + [ANY] * len(after),
        compiler_params=params(),
        cost_estimate=estimate,
    )(target, *blocks, *after)
    got = [lax.ppermute(part, "dp", [(j, j ^ 1) for j in range(dp_size)]) for part in other]
    own = pl.pallas_call(
        pack_own_kernel,
        out_shape=jax.ShapeDtypeStruct((half, wide), jnp.bfloat16),
        compiler_params=params(),
        cost_estimate=estimate,
    )(target, *blocks)
    outs = pl.pallas_call(
        merge_kernel,
        out_shape=[jax.ShapeDtypeStruct((2 * capacity, wide), jnp.bfloat16)] * (dp_size // 2),
        compiler_params=params(),
        cost_estimate=cost(0, 8 * half * wide),
    )(own, *got)
    return swap(list(outs), "dp", dp_size, 2)


def attend_kernel(
    heads, doc_most, ctx_size, number, waits, with_kv, *refs
):
    slot_ref, live_ref, doc_ref, col_ref = refs[:4]
    blocks, refs = refs[4 : 4 + number], refs[4 + number + waits :]
    if with_kv:
        outs, kv_ref, acc = refs[:-2], refs[-2], refs[-1]
    else:
        kv_ref, outs, acc = refs[0], refs[1:-1], refs[-1]
    me = lax.axis_index("ctx")
    pack_len = acc.shape[0]
    wide = heads * HEAD_DIM
    scale = HEAD_DIM ** (-0.5) * math.log2(math.e)
    window = min(pack_len, doc_most + BLOCK)
    live = live_ref[...]
    ones = jnp.ones((window, HEAD_DIM), jnp.bfloat16)
    received = rows_of(blocks)
    most = 6 * BLOCK
    row = lax.broadcasted_iota(jnp.int32, (most, pack_len), 0)
    for begin in range(0, pack_len, most):
        place = jnp.where(slot_ref[...] == row + begin, 1.0, 0.0).astype(jnp.bfloat16)
        packed = jnp.dot(place, received, preferred_element_type=jnp.float32).astype(jnp.bfloat16)
        acc[begin : begin + most, :] = packed[:, :wide]
        if with_kv:
            kv_ref[begin : begin + most, :] = packed[:, wide:]
    for block in range(pack_len // BLOCK):
        begin = block * BLOCK
        rows = pl.ds(begin, BLOCK)
        packed = acc[rows, :]
        key_start = max(0, begin + BLOCK - window)
        span = begin + BLOCK - key_start
        keys = kv_ref[pl.ds(key_start, span), :HEAD_DIM]
        values = jnp.concatenate([kv_ref[pl.ds(key_start, span), HEAD_DIM:], ones[:span]], axis=1)
        query_pos = begin + lax.broadcasted_iota(jnp.int32, (BLOCK, span), 0)
        key_pos = key_start + lax.broadcasted_iota(jnp.int32, (BLOCK, span), 1)
        docs = jnp.concatenate([col_ref[rows, :]] * (span // HEAD_DIM), axis=1)
        allowed = (docs == doc_ref[:, pl.ds(key_start, span)]) & (key_pos <= query_pos)
        bias = jnp.where(allowed, 0.0, -1e30)
        alive = begin + lax.broadcasted_iota(jnp.int32, (BLOCK, HEAD_DIM), 0) < live
        queries = jnp.concatenate(
            [packed[:, i * HEAD_DIM : (i + 1) * HEAD_DIM] for i in range(heads)], axis=0
        )
        scores = lax.dot_general(
            queries, keys, (((1,), (1,)), ((), ())), preferred_element_type=jnp.float32
        )
        masked = scores.reshape(heads, BLOCK, span) + bias[None]
        top = jnp.max(masked, axis=2, keepdims=True)
        weights = jnp.exp2((masked - top) * scale).astype(jnp.bfloat16)
        mixed = jnp.dot(
            weights.reshape(heads * BLOCK, span), values, preferred_element_type=jnp.float32
        )
        result = mixed[:, :HEAD_DIM] / mixed[:, HEAD_DIM:]
        for i in range(heads):
            head = jnp.where(alive, result[i * BLOCK : (i + 1) * BLOCK], 0.0)
            acc[rows, i * HEAD_DIM : (i + 1) * HEAD_DIM] = head.astype(jnp.bfloat16)
    part = pack_len // ctx_size
    for step in range(ctx_size):
        first = pl.multiple_of((me ^ step) * part, part)
        outs[step][...] = acc[pl.ds(first, part), :]


def attend(received, slot, live, doc_row, doc_col, kv, heads, ctx_size, after):
    pack_len = slot.shape[1]
    doc_most = pack_len // 3
    wide = heads * HEAD_DIM
    with_kv = kv is None
    part = pack_len // ctx_size
    shapes = [jax.ShapeDtypeStruct((part, wide), jnp.bfloat16)] * ctx_size
    sent = len(shapes)
    if with_kv:
        shapes = shapes + [jax.ShapeDtypeStruct((pack_len, 2 * HEAD_DIM), jnp.bfloat16)]
    work = pack_len * (doc_most + BLOCK) * heads
    outs = pl.pallas_call(
        functools.partial(
            attend_kernel,
            heads,
            doc_most,
            ctx_size,
            len(received),
            len(after),
            with_kv,
        ),
        out_shape=shapes,
        in_specs=[VMEM] * (4 + len(received)) + [ANY] * len(after) + [VMEM] * (0 if with_kv else 1),
        scratch_shapes=[pltpu.VMEM((pack_len, wide), jnp.bfloat16)],
        compiler_params=params(),
        cost_estimate=cost(
            2 * pack_len * pack_len * received[0].shape[1] + 6 * work * HEAD_DIM,
            8 * pack_len * wide,
            work,
        ),
    )(slot, live, doc_row, doc_col, *received, *after, *([] if with_kv else [kv]))
    return list(outs[:sent]), (outs[sent] if with_kv else kv)


def join_kernel(chunk, ctx_size, steps, *refs):
    offset, heads = chunk
    heads_dev = Q_HEADS // ctx_size
    out, sem = refs[-2:]
    me = lax.axis_index("ctx")
    copies = []
    for at, step in enumerate(steps):
        column = pl.multiple_of(((me ^ step) * heads_dev + offset) * HEAD_DIM, HEAD_DIM)
        copies.append(
            pltpu.make_async_copy(
                refs[at], out.at[:, pl.ds(column, heads * HEAD_DIM)], sem.at[at]
            )
        )
    for copy in copies:
        copy.start()
    for copy in copies:
        copy.wait()


def join(blocks, chunk, out, ctx_size):
    rows = blocks[0].shape[0]
    given = [] if out is None else [out]
    steps = JOIN_ORDER if len(JOIN_ORDER) == ctx_size else tuple(range(ctx_size))
    return pl.pallas_call(
        functools.partial(join_kernel, chunk, ctx_size, steps),
        out_shape=jax.ShapeDtypeStruct((rows, Q_HEADS * HEAD_DIM), jnp.bfloat16),
        in_specs=[ANY] * (ctx_size + len(given)),
        out_specs=ANY,
        scratch_shapes=[pltpu.SemaphoreType.DMA((ctx_size,))],
        input_output_aliases={ctx_size: 0} if given else {},
        compiler_params=params(),
        cost_estimate=cost(0, 4 * rows * chunk[1] * HEAD_DIM * ctx_size),
    )(*[blocks[step] for step in steps], *given)


def on_device(q_src, kv_src, route, doc_ids):
    ctx_size = lax.axis_size("ctx")
    dp_size = lax.axis_size("dp")
    length = q_src.shape[0] * ctx_size
    capacity = 3 * length // (2 * dp_size)
    pack_len = dp_size * capacity
    chunks = head_chunks(Q_HEADS // ctx_size)

    gathered, after = [], []
    for at, chunk in enumerate(chunks):
        blocks = cut(q_src, kv_src, chunk, ctx_size, at == 0, after)
        gathered.append(swap(blocks, "ctx", ctx_size))
        after = blocks[:1]
    doc_col = jnp.broadcast_to(doc_ids.reshape(pack_len, 1), (pack_len, HEAD_DIM))
    target, slot, live = plan(route, dp_size, ctx_size, capacity, doc_col)

    packed = []
    for at, blocks in enumerate(gathered):
        after = [blocks[1] for blocks in gathered[at + 1 : at + 2]] + [p[0] for p in packed[-1:]]
        packed.append(deliver(target, blocks, dp_size, capacity, after))

    kv, sends = None, []
    for at, chunk in enumerate(chunks):
        after = [sends[-1][0]] if sends else [p[0] for p in packed[1:2]]
        blocks, kv = attend(
            packed[at], slot, live, doc_ids, doc_col, kv, chunk[1], ctx_size, after
        )
        sends.append(swap(blocks, "ctx", ctx_size))
    out = None
    for chunk, blocks in zip(chunks, sends):
        out = join(blocks, chunk, out, ctx_size)
    return out


def solution(mesh):
    in_specs = (P(("dp", "ctx"), None), P(("dp", "ctx"), None), P(), P("dp", None))
    out_specs = P(("dp", "ctx"), None)
    return jax.shard_map(
        on_device, mesh=mesh, in_specs=in_specs, out_specs=out_specs, check_vma=False
    )
```

```python
import functools
import math

import jax
import jax.numpy as jnp
from jax import lax
from jax.experimental import pallas as pl
from jax.experimental.pallas import tpu as pltpu
from jax.sharding import PartitionSpec as P

Q_HEADS = 32
KV_HEADS = 4
HEAD_DIM = 128
BLOCK = 128
VMEM_LIMIT = 40 * 1024 * 1024
SWAPS = 2
JOIN_ORDER = (2, 3, 1, 0)
ANY = pl.BlockSpec(memory_space=pl.ANY)
VMEM = pl.BlockSpec(memory_space=pltpu.VMEM)


def params():
    return pltpu.CompilerParams(vmem_limit_bytes=VMEM_LIMIT)


def cost(flops, moved, exps=0):
    return pl.CostEstimate(flops=int(flops), bytes_accessed=int(moved), transcendentals=int(exps))


def head_chunks(heads_dev):
    first = max(1, heads_dev // 2)
    return [(0, first)] + ([(first, heads_dev - first)] if heads_dev > first else [])


def cut_kernel(chunk, ctx_size, with_kv, waits, q_ref, *refs):
    offset, heads = chunk
    kv_ref, refs = (refs[0], refs[1:]) if with_kv else (None, refs)
    outs, sem = refs[waits:-1], refs[-1]
    me = lax.axis_index("ctx")
    heads_dev = Q_HEADS // ctx_size
    group = Q_HEADS // KV_HEADS
    copies = []
    for step in list(range(1, ctx_size)) + [0]:
        owner = me ^ step
        parts = [(q_ref, owner * heads_dev + offset, heads)]
        if with_kv:
            head = (owner * heads_dev) // group
            parts += [(kv_ref, head, 1), (kv_ref, KV_HEADS + head, 1)]
        place = 0
        for source, block, number in parts:
            wide = number * HEAD_DIM
            column = pl.multiple_of(block * HEAD_DIM, HEAD_DIM)
            copies.append(
                (source.at[:, pl.ds(column, wide)], outs[step].at[:, pl.ds(place, wide)])
            )
            place += wide
    started = [pltpu.make_async_copy(a, b, sem.at[i]) for i, (a, b) in enumerate(copies)]
    for copy in started:
        copy.start()
    for copy in started:
        copy.wait()


def cut(q_src, kv_src, chunk, ctx_size, with_kv, after):
    rows = q_src.shape[0]
    wide = (chunk[1] + (2 if with_kv else 0)) * HEAD_DIM
    shapes = [jax.ShapeDtypeStruct((rows, wide), jnp.bfloat16)] * ctx_size
    sources = [q_src, kv_src] if with_kv else [q_src]
    sources = [pltpu.with_memory_space_constraint(x, pltpu.HBM) for x in sources]
    outs = pl.pallas_call(
        functools.partial(cut_kernel, chunk, ctx_size, with_kv, len(after)),
        out_shape=shapes,
        in_specs=[ANY] * (len(sources) + len(after)),
        out_specs=[VMEM] * len(shapes),
        scratch_shapes=[pltpu.SemaphoreType.DMA((ctx_size * (3 if with_kv else 1),))],
        compiler_params=params(),
        cost_estimate=cost(0, 4 * ctx_size * rows * wide),
    )(*sources, *after)
    return list(outs)


def swap(blocks, axis, size, unit=1):
    return [blocks[0]] + [
        lax.ppermute(blocks[step], axis, [(j, j ^ (step * unit)) for j in range(size)])
        for step in range(1, len(blocks))
    ]


def plan_kernel(capacity, ctx_size, route_ref, _, target_ref, slot_ref, live_ref, natural):
    dp_size, length = route_ref.shape
    rows = length // ctx_size
    pack_len = dp_size * capacity
    own, me = lax.axis_index("dp"), lax.axis_index("ctx")
    mine = route_ref[pl.ds(own, 1), :]
    seq = lax.broadcasted_iota(jnp.int32, (dp_size, length), 0)
    onehot = jnp.where(mine == seq, 1.0, 0.0)
    earlier = lax.broadcasted_iota(jnp.int32, (length, length), 0)
    later = lax.broadcasted_iota(jnp.int32, (length, length), 1)
    strict = jnp.where(earlier < later, 1.0, 0.0).astype(jnp.bfloat16)
    before = jnp.dot(onehot.astype(jnp.bfloat16), strict, preferred_element_type=jnp.float32)
    rank = jnp.sum(before * onehot, axis=0, keepdims=True).astype(jnp.int32)
    other = mine ^ own
    place = (other & 1) * (dp_size // 2) + (other >> 1)
    natural[...] = place * capacity + rank
    for step in range(ctx_size):
        source = me ^ step
        target_ref[:, pl.ds(step * rows, rows)] = natural[
            :, pl.ds(pl.multiple_of(source * rows, rows), rows)
        ]
    incoming = jnp.sum(
        jnp.where(route_ref[...] == own, 1.0, 0.0), axis=1, keepdims=True
    )
    group = lax.broadcasted_iota(jnp.int32, (dp_size, pack_len), 0)
    lane = lax.broadcasted_iota(jnp.int32, (dp_size, pack_len), 1)
    block = lax.div(lane, capacity)
    source = block ^ own
    start = jnp.sum(jnp.where(group < source, incoming, 0.0), axis=0, keepdims=True)
    amount = jnp.sum(jnp.where(group == source, incoming, 0.0), axis=0, keepdims=True)
    offset = (lane - block * capacity)[:1]
    slot_ref[...] = jnp.where(
        offset < amount.astype(jnp.int32), start.astype(jnp.int32) + offset, -1
    )
    live = jnp.sum(incoming, axis=0, keepdims=True).astype(jnp.int32)
    live_ref[...] = jnp.broadcast_to(live, live_ref.shape)


def plan(route, dp_size, ctx_size, capacity, after):
    length = route.shape[0] // dp_size
    return pl.pallas_call(
        functools.partial(plan_kernel, capacity, ctx_size),
        out_shape=[
            jax.ShapeDtypeStruct((1, length), jnp.int32),
            jax.ShapeDtypeStruct((1, dp_size * capacity), jnp.int32),
            jax.ShapeDtypeStruct((1, HEAD_DIM), jnp.int32),
        ],
        in_specs=[VMEM, ANY],
        scratch_shapes=[pltpu.VMEM((1, length), jnp.int32)],
        compiler_params=params(),
        cost_estimate=cost(2 * dp_size * length * length, 8 * length * dp_size),
    )(route.reshape(dp_size, length), after)


def rows_of(blocks):
    return jnp.concatenate([b[...] for b in blocks], axis=0)


def place_rows(target_ref, data, begin, count):
    row = begin + lax.broadcasted_iota(jnp.int32, (count, target_ref.shape[1]), 0)
    place = jnp.where(target_ref[...] == row, 1.0, 0.0).astype(jnp.bfloat16)
    return jnp.dot(place, data, preferred_element_type=jnp.float32).astype(jnp.bfloat16)


def pack_other_kernel(number, target_ref, *refs):
    outs = refs[-SWAPS:]
    size = outs[0].shape[0]
    half = size * SWAPS
    packed = place_rows(target_ref, rows_of(refs[:number]), half, half)
    for at, out in enumerate(outs):
        out[...] = packed[at * size : (at + 1) * size]


def pack_own_kernel(target_ref, *refs):
    refs[-1][...] = place_rows(target_ref, rows_of(refs[:-1]), 0, refs[-1].shape[0])


def merge_kernel(own_ref, *refs):
    got, outs = refs[:SWAPS], refs[SWAPS:]
    size = got[0].shape[0]
    capacity = outs[0].shape[0] // 2
    for step, out in enumerate(outs):
        first = step * capacity
        out[:capacity, :] = own_ref[first : first + capacity, :]
        begin = first % size
        out[capacity:, :] = got[first // size][begin : begin + capacity, :]


def deliver(target, blocks, dp_size, capacity, after):
    wide = blocks[0].shape[-1]
    length = target.shape[1]
    half = dp_size // 2 * capacity
    estimate = cost(2 * half * length * wide, 2 * (half + length) * wide)
    other = pl.pallas_call(
        functools.partial(pack_other_kernel, len(blocks)),
        out_shape=[jax.ShapeDtypeStruct((half // SWAPS, wide), jnp.bfloat16)] * SWAPS,
        in_specs=[VMEM] * (1 + len(blocks)) + [ANY] * len(after),
        compiler_params=params(),
        cost_estimate=estimate,
    )(target, *blocks, *after)
    got = [lax.ppermute(part, "dp", [(j, j ^ 1) for j in range(dp_size)]) for part in other]
    own = pl.pallas_call(
        pack_own_kernel,
        out_shape=jax.ShapeDtypeStruct((half, wide), jnp.bfloat16),
        compiler_params=params(),
        cost_estimate=estimate,
    )(target, *blocks)
    outs = pl.pallas_call(
        merge_kernel,
        out_shape=[jax.ShapeDtypeStruct((2 * capacity, wide), jnp.bfloat16)] * (dp_size // 2),
        compiler_params=params(),
        cost_estimate=cost(0, 8 * half * wide),
    )(own, *got)
    return swap(list(outs), "dp", dp_size, 2)


def attend_kernel(
    heads, doc_most, ctx_size, number, waits, with_kv, *refs
):
    slot_ref, live_ref, doc_ref, col_ref = refs[:4]
    blocks, refs = refs[4 : 4 + number], refs[4 + number + waits :]
    if with_kv:
        outs, kv_ref, acc = refs[:-2], refs[-2], refs[-1]
    else:
        kv_ref, outs, acc = refs[0], refs[1:-1], refs[-1]
    me = lax.axis_index("ctx")
    pack_len = acc.shape[0]
    wide = heads * HEAD_DIM
    scale = HEAD_DIM ** (-0.5) * math.log2(math.e)
    window = min(pack_len, doc_most + BLOCK)
    live = live_ref[...]
    ones = jnp.ones((window, HEAD_DIM), jnp.bfloat16)
    received = rows_of(blocks)
    most = 6 * BLOCK
    row = lax.broadcasted_iota(jnp.int32, (most, pack_len), 0)
    for begin in range(0, pack_len, most):
        place = jnp.where(slot_ref[...] == row + begin, 1.0, 0.0).astype(jnp.bfloat16)
        packed = jnp.dot(place, received, preferred_element_type=jnp.float32).astype(jnp.bfloat16)
        acc[begin : begin + most, :] = packed[:, :wide]
        if with_kv:
            kv_ref[begin : begin + most, :] = packed[:, wide:]
    for block in range(pack_len // BLOCK):
        begin = block * BLOCK
        rows = pl.ds(begin, BLOCK)
        packed = acc[rows, :]
        key_start = max(0, begin + BLOCK - window)
        span = begin + BLOCK - key_start
        keys = kv_ref[pl.ds(key_start, span), :HEAD_DIM]
        values = jnp.concatenate([kv_ref[pl.ds(key_start, span), HEAD_DIM:], ones[:span]], axis=1)
        query_pos = begin + lax.broadcasted_iota(jnp.int32, (BLOCK, span), 0)
        key_pos = key_start + lax.broadcasted_iota(jnp.int32, (BLOCK, span), 1)
        docs = jnp.concatenate([col_ref[rows, :]] * (span // HEAD_DIM), axis=1)
        allowed = (docs == doc_ref[:, pl.ds(key_start, span)]) & (key_pos <= query_pos)
        bias = jnp.where(allowed, 0.0, -1e30)
        alive = begin + lax.broadcasted_iota(jnp.int32, (BLOCK, HEAD_DIM), 0) < live
        queries = jnp.concatenate(
            [packed[:, i * HEAD_DIM : (i + 1) * HEAD_DIM] for i in range(heads)], axis=0
        )
        scores = lax.dot_general(
            queries, keys, (((1,), (1,)), ((), ())), preferred_element_type=jnp.float32
        )
        masked = scores.reshape(heads, BLOCK, span) + bias[None]
        top = jnp.max(masked, axis=2, keepdims=True)
        weights = jnp.exp2((masked - top) * scale).astype(jnp.bfloat16)
        mixed = jnp.dot(
            weights.reshape(heads * BLOCK, span), values, preferred_element_type=jnp.float32
        )
        result = mixed[:, :HEAD_DIM] / mixed[:, HEAD_DIM:]
        for i in range(heads):
            head = jnp.where(alive, result[i * BLOCK : (i + 1) * BLOCK], 0.0)
            acc[rows, i * HEAD_DIM : (i + 1) * HEAD_DIM] = head.astype(jnp.bfloat16)
    part = pack_len // ctx_size
    for step in range(ctx_size):
        first = pl.multiple_of((me ^ step) * part, part)
        outs[step][...] = acc[pl.ds(first, part), :]


def attend(received, slot, live, doc_row, doc_col, kv, heads, ctx_size, after):
    pack_len = slot.shape[1]
    doc_most = pack_len // 3
    wide = heads * HEAD_DIM
    with_kv = kv is None
    part = pack_len // ctx_size
    shapes = [jax.ShapeDtypeStruct((part, wide), jnp.bfloat16)] * ctx_size
    sent = len(shapes)
    if with_kv:
        shapes = shapes + [jax.ShapeDtypeStruct((pack_len, 2 * HEAD_DIM), jnp.bfloat16)]
    work = pack_len * (doc_most + BLOCK) * heads
    outs = pl.pallas_call(
        functools.partial(
            attend_kernel,
            heads,
            doc_most,
            ctx_size,
            len(received),
            len(after),
            with_kv,
        ),
        out_shape=shapes,
        in_specs=[VMEM] * (4 + len(received)) + [ANY] * len(after) + [VMEM] * (0 if with_kv else 1),
        scratch_shapes=[pltpu.VMEM((pack_len, wide), jnp.bfloat16)],
        compiler_params=params(),
        cost_estimate=cost(
            2 * pack_len * pack_len * received[0].shape[1] + 6 * work * HEAD_DIM,
            8 * pack_len * wide,
            work,
        ),
    )(slot, live, doc_row, doc_col, *received, *after, *([] if with_kv else [kv]))
    return list(outs[:sent]), (outs[sent] if with_kv else kv)


def join_kernel(chunk, ctx_size, steps, *refs):
    offset, heads = chunk
    heads_dev = Q_HEADS // ctx_size
    out, sem = refs[-2:]
    me = lax.axis_index("ctx")
    copies = []
    for at, step in enumerate(steps):
        column = pl.multiple_of(((me ^ step) * heads_dev + offset) * HEAD_DIM, HEAD_DIM)
        copies.append(
            pltpu.make_async_copy(
                refs[at], out.at[:, pl.ds(column, heads * HEAD_DIM)], sem.at[at]
            )
        )
    for copy in copies:
        copy.start()
    for copy in copies:
        copy.wait()


def join(blocks, chunk, out, ctx_size):
    rows = blocks[0].shape[0]
    given = [] if out is None else [out]
    steps = JOIN_ORDER if len(JOIN_ORDER) == ctx_size else tuple(range(ctx_size))
    return pl.pallas_call(
        functools.partial(join_kernel, chunk, ctx_size, steps),
        out_shape=jax.ShapeDtypeStruct((rows, Q_HEADS * HEAD_DIM), jnp.bfloat16),
        in_specs=[ANY] * (ctx_size + len(given)),
        out_specs=ANY,
        scratch_shapes=[pltpu.SemaphoreType.DMA((ctx_size,))],
        input_output_aliases={ctx_size: 0} if given else {},
        compiler_params=params(),
        cost_estimate=cost(0, 4 * rows * chunk[1] * HEAD_DIM * ctx_size),
    )(*[blocks[step] for step in steps], *given)


def on_device(q_src, kv_src, route, doc_ids):
    ctx_size = lax.axis_size("ctx")
    dp_size = lax.axis_size("dp")
    length = q_src.shape[0] * ctx_size
    capacity = 3 * length // (2 * dp_size)
    pack_len = dp_size * capacity
    chunks = head_chunks(Q_HEADS // ctx_size)

    gathered, after = [], []
    for at, chunk in enumerate(chunks):
        blocks = cut(q_src, kv_src, chunk, ctx_size, at == 0, after)
        gathered.append(swap(blocks, "ctx", ctx_size))
        after = blocks[:1]
    doc_col = jnp.broadcast_to(doc_ids.reshape(pack_len, 1), (pack_len, HEAD_DIM))
    target, slot, live = plan(route, dp_size, ctx_size, capacity, doc_col)

    packed = []
    for at, blocks in enumerate(gathered):
        after = [blocks[1] for blocks in gathered[at + 1 : at + 2]] + [p[0] for p in packed[-1:]]
        packed.append(deliver(target, blocks, dp_size, capacity, after))

    kv, sends = None, []
    for at, chunk in enumerate(chunks):
        after = [] if sends else []
        blocks, kv = attend(
            packed[at], slot, live, doc_ids, doc_col, kv, chunk[1], ctx_size, after
        )
        sends.append(swap(blocks, "ctx", ctx_size))
    out = None
    for chunk, blocks in zip(chunks, sends):
        out = join(blocks, chunk, out, ctx_size)
    return out


def solution(mesh):
    in_specs = (P(("dp", "ctx"), None), P(("dp", "ctx"), None), P(), P("dp", None))
    out_specs = P(("dp", "ctx"), None)
    return jax.shard_map(
        on_device, mesh=mesh, in_specs=in_specs, out_specs=out_specs, check_vma=False
    )
```
